128 devices in a mesh: tx: 8 (over z, x_lo), ty: 4 (over y), mem: 4 (over x_hi, core).
Axes of the slice: x: 4 (x_hi: 2, x_lo: 2; x = x_hi * 2 + x_lo), y: 4, z: 4, core: 2. Of those that a mesh axis runs over, the one named last changes fastest.
Arguments:
- alpha: float32 [64, 128, 2560], P('tx', 'ty', 'mem'), may hold values from -6 to 6
- lv_sqrt: float32 [32, 32], replicated, may hold values from -1 to 1
- ens_pert: bfloat16 [80, 32, 256, 512], P('mem', None, 'tx', 'ty'), may hold values from -0.625 to 0.625
- bg_sigma: float32 [32, 256, 512], P(None, 'tx', 'ty'), may hold values from 0.1 to 1
- static_ctrl: float32 [32, 256, 512], P(None, 'tx', 'ty'), may hold values from -6 to 6
- obs_owner: int32 [1048576, 1], P(('tx', 'ty', 'mem')), may hold values from 0 to 31; in each aligned block of 8192 rows (0 to 8191, 8192 to 16383, ...) at most 512 rows name the same one
- obs_column: int32 [1048576], P(('tx', 'ty', 'mem')), may hold values from 0 to 3966, as said below
- obs_level: int32 [1048576], P(('tx', 'ty', 'mem')), may hold values from 0 to 30
- obs_frac: float32 [3, 1048576], P(None, ('tx', 'ty', 'mem')), may hold values from 0 to 1
- innovation: float32 [1048576], P(('tx', 'ty', 'mem')), may hold values from -6 to 6
- obs_rinv: float32 [1048576], P(('tx', 'ty', 'mem')), may hold values from 0.5 to 8
- obs_count: int32 [128], P(('tx', 'ty', 'mem')), may hold values from 4096 to 8192, as said below
Outputs:
- grad_alpha: float32 [64, 128, 2560], P('tx', 'ty', 'mem')
- grad_static: float32 [32, 256, 512], P(None, 'tx', 'ty')
- departures: float32 [1048576], P(('tx', 'ty', 'mem'))
The draws below stay inside these ranges and needn't reach their ends.
Inputs may be any that keep to these rules, and one draw needn't show every extreme that they name: `obs_owner`: tile number (tx index) * 4 + (ty index). Among one device's 8192 rows no tile is named more than 512 times, a bound that some block reaches. `obs_column`: i * 128 + j with i < 31 and j < 127. `obs_count`: the live slots of a device are its first ones; some device has all 8192 live and some half of them.
All inputs are finite; a program needn't handle non-finite values.
Results may differ from the reference program's by a relative error of at most 0.0003.
Values sent between devices are 32-bit elements; how exact they have to be, the bound alone decides.
A program may use at most 128 MiB of HBM per device.

```python
import math
import jax
import jax.numpy as jnp
import numpy as np
from jax import lax

MEMBERS = 80
LEV = 32
FX = 32
FY = 128
RATIO = 4
NSTEP = 4
OBS_DEV = 8192
NFX = 256
NFY = 512
NCX = 64
NCY = 128
TILES = 32
NOBS = 1048576
CAP = 512
N_TY = 4
DEVICES = 128


def draw_obs_column(key, part):
    key = jax.random.fold_in(key, 11)
    first, second = jax.random.split(key)
    across = jax.random.randint(first, (NOBS,), 0, FX - 1)
    along = jax.random.randint(second, (NOBS,), 0, FY - 1)
    across = across.at[0].set(FX - 2)
    along = along.at[0].set(FY - 2)
    return (across * FY + along).astype(jnp.int32)


def draw_obs_count(key, part):
    key = jax.random.fold_in(key, 12)
    counts = jax.random.randint(key, (DEVICES,), OBS_DEV // 2, OBS_DEV + 1)
    counts = counts.at[0].set(OBS_DEV).at[1].set(OBS_DEV // 2)
    return counts.astype(jnp.int32)


def touch_ends(values, rng, smallest, largest):
    longest = values.shape.index(max(values.shape))
    spots = []
    for shift in (0, 1):
        where = [jax.random.randint(jax.random.fold_in(rng, axis), (), 0, length) for axis, length in enumerate(values.shape)]
        where[longest] = (where[longest] + shift) % values.shape[longest]
        spots.append(tuple(where))
    return values.at[spots[0]].set(smallest).at[spots[1]].set(largest)


def levels(rng, dims, cuts, smallest, high):
    def one(axis_at, parts):
        heights = jax.random.uniform(jax.random.fold_in(jax.random.fold_in(rng, 6), axis_at), (parts,), jnp.float32, smallest / len(cuts), high / len(cuts))
        return jnp.repeat(jnp.exp(heights), dims[axis_at] // parts).reshape((-1,) + (1,) * (len(dims) - axis_at - 1))

    factor_of = one(*cuts[0])
    for cut in cuts[1:]:
        factor_of = factor_of * one(*cut)
    return factor_of


def deal_out(rng, own, number, rows, amount, top, bound, slope):
    order = jax.random.permutation(rng, amount)
    heavy_load, ordinary = load_shares(amount, rows * top, bound, slope, True), load_shares(amount, rows * top, bound, slope, False)
    places = jnp.arange(amount)

    def named(sizes, turn):
        used = int((sizes > 0).sum())
        fixed = max(1, used // 4)
        moved = fixed + (places - fixed + turn * (used - fixed)) % max(1, amount - fixed)
        return jnp.zeros((amount,), jnp.int32).at[order[jnp.where(places < fixed, places, moved)]].set(jnp.asarray(sizes, jnp.int32))

    sizes = jnp.where(number % 4 == 0, named(heavy_load, number // 4), named(ordinary, number - number // 4 - 1))
    mixed = jax.random.permutation(jax.random.fold_in(own, 3), amount)
    giver, sink = mixed[0:amount // 2 * 2:2], mixed[1:amount // 2 * 2:2]
    slack = jnp.minimum(sizes[giver] - 1, bound - sizes[sink]) // 2
    slack = jnp.where((giver == order[0]) | (sink == order[0]) | (sizes[sink] == 0), 0, jnp.maximum(slack, 0))
    moved = jax.random.randint(jax.random.fold_in(own, 4), (amount // 2,), 0, 1 << 20) % (slack + 1)
    sizes = sizes.at[giver].add(-moved).at[sink].add(moved)
    labels = jnp.searchsorted(jnp.cumsum(sizes), jnp.arange(rows * top), side="right").astype(jnp.int32)
    listing = labels.reshape(top, rows).T
    listing = listing[jax.random.permutation(jax.random.fold_in(own, 1), rows)]
    turn = jax.random.randint(jax.random.fold_in(own, 2), (rows, 1), 0, top)
    return jnp.take_along_axis(listing, (jnp.arange(top)[None, :] + turn) % top, axis=1)


def load_shares(amount, total, most, slope, full):
    weights = [(1 << 20) // math.isqrt(standing ** slope) + 1 for standing in range(1, amount + 1)]
    largest = most if full else min(most, max(-(-total // amount), total * weights[0] // sum(weights)))
    least = 1 if total - largest >= amount - 1 else 0
    given, rest = [largest] + [least] * (amount - 1), total - largest - least * (amount - 1)
    while rest > 0:
        candidates = [i for i in range(1, amount) if given[i] < largest] or [i for i in range(1, amount) if given[i] < most]
        pool, remaining = sum([weights[i] for i in candidates]), rest
        for i in candidates:
            extra = min(most - given[i], max(1, remaining * weights[i] // pool), rest)
            given[i] = given[i] + extra
            rest = rest - extra
    return np.array(given)


def centred(key, dims, scale, reach, shards=(), kind=jnp.bfloat16):
    values = scale * jax.random.normal(key, dims, jnp.float32)
    if shards:
        values = values * levels(key, dims, shards, -0.22, 0.18)
    return jnp.clip(values, -reach, reach).astype(kind)


def setup_inputs(seed: int = 0) -> dict:
    splits = jax.random.split(jax.random.key(seed), 13)
    alpha = centred(splits[0], (NCX, NCY, MEMBERS * LEV), 1.0, 6.0, ((0, 8), (1, 4), (2, 4)), jnp.float32)
    lv_sqrt = centred(splits[1], (LEV, LEV), LEV ** -0.5, 1.0, (), jnp.float32)
    ens_pert = centred(splits[2], (MEMBERS, LEV, NFX, NFY), MEMBERS ** -0.5, 0.625, ((0, 4), (2, 8), (3, 4)))
    bg_sigma = jnp.clip(jnp.exp(math.log(1.0) - 2.3025851 * jax.random.uniform(splits[3], (LEV, NFX, NFY), jnp.float32) ** levels(splits[3], (LEV, NFX, NFY), ((1, 8), (2, 4)), -0.2, 0.2)), 0.1, 1.0)
    static_ctrl = centred(splits[4], (LEV, NFX, NFY), 1.0, 6.0, ((1, 8), (2, 4)), jnp.float32)
    obs_owner_keys = jax.random.split(jax.random.fold_in(splits[5], 1), NOBS // OBS_DEV)
    obs_owner_turns = jax.random.permutation(jax.random.fold_in(splits[5], 3), NOBS // OBS_DEV)
    obs_owner = jax.vmap(lambda own, number: deal_out(jax.random.fold_in(splits[5], 2), own, number, OBS_DEV, TILES, 1, CAP, 1))(obs_owner_keys, obs_owner_turns).reshape((NOBS, 1))
    obs_column = draw_obs_column(jax.random.fold_in(splits[12], 71), 0)
    obs_level = touch_ends(jax.random.randint(splits[7], (NOBS,), 0, LEV - 1), jax.random.fold_in(splits[7], 1), 0, (LEV - 1) - 1).astype(jnp.int32)
    obs_frac = jnp.clip(1.0 * jax.random.uniform(splits[8], (3, NOBS), jnp.float32) ** levels(splits[8], (3, NOBS), ((1, 128),), -0.2, 0.2), 0.0, 1.0)
    innovation = centred(splits[9], (NOBS,), 1.0, 6.0, ((0, 128),), jnp.float32)
    obs_rinv = jnp.clip(jnp.exp(math.log(8.0) - 2.7725887 * jax.random.uniform(splits[10], (NOBS,), jnp.float32) ** levels(splits[10], (NOBS,), ((0, 128),), -0.2, 0.2)), 0.5, 8.0)
    obs_count = draw_obs_count(jax.random.fold_in(splits[12], 71), 0)
    return {"alpha": alpha, "lv_sqrt": lv_sqrt, "ens_pert": ens_pert, "bg_sigma": bg_sigma, "static_ctrl": static_ctrl, "obs_owner": obs_owner, "obs_column": obs_column, "obs_level": obs_level, "obs_frac": obs_frac, "innovation": innovation, "obs_rinv": obs_rinv, "obs_count": obs_count}


NU = 0.2

def diffuse(field):
    for repeat in range(NSTEP):
        near = jnp.roll(field, 1, 0) + jnp.roll(field, -1, 0) + jnp.roll(field, 1, 1) + jnp.roll(field, -1, 1)
        field = field + NU * (near - 4.0 * field)
    return field

def upsample(coarse):
    frac = jnp.arange(RATIO, dtype=jnp.float32) / RATIO
    first = (1.0 - frac)[None, :, None, None] * coarse[:, None] + frac[None, :, None, None] * jnp.roll(coarse, -1, 0)[:, None]
    first = first.reshape(NFX, NCY, LEV)
    second = (1.0 - frac)[None, None, :, None] * first[:, :, None] + frac[None, None, :, None] * jnp.roll(first, -1, 1)[:, :, None]
    second = second.reshape(NFX, NFY, LEV)
    return jnp.transpose(second, (2, 0, 1))

def coarsen_field(fine_grid):
    frac = jnp.arange(RATIO, dtype=jnp.float32) / RATIO
    grid = jnp.transpose(fine_grid, (1, 2, 0))
    grid = grid.reshape(NFX, NCY, RATIO, LEV)
    lower = lax.optimization_barrier(jnp.sum((1.0 - frac)[None, None, :, None] * grid, 2))
    upper = lax.optimization_barrier(jnp.sum(frac[None, None, :, None] * grid, 2))
    grid = lower + jnp.roll(upper, 1, 1)
    grid = grid.reshape(NCX, RATIO, NCY, LEV)
    lower = lax.optimization_barrier(jnp.sum((1.0 - frac)[None, :, None, None] * grid, 1))
    upper = lax.optimization_barrier(jnp.sum(frac[None, :, None, None] * grid, 1))
    return lower + jnp.roll(upper, 1, 0)

def reference(alpha, lv_sqrt, ens_pert, bg_sigma, static_ctrl, obs_owner, obs_column, obs_level, obs_frac, innovation, obs_rinv, obs_count):
    highest = lax.Precision.HIGHEST
    alpha_four = alpha.reshape(NCX, NCY, MEMBERS, LEV)
    vert = jnp.einsum('xykm,lm->xykl', alpha_four, lv_sqrt, precision=highest)
    smooth = jnp.moveaxis(diffuse(vert), 2, 0)

    def forward(total, pair):
        coarse, member_perturbation = pair
        return (total + upsample(coarse) * member_perturbation.astype(jnp.float32), None)
    increment, unused = lax.scan(forward, jnp.zeros((LEV, NFX, NFY), jnp.float32), (smooth, ens_pert))
    increment = increment + bg_sigma * static_ctrl
    grid_position = jnp.arange(NOBS, dtype=jnp.int32)
    device = grid_position // OBS_DEV
    live = grid_position % OBS_DEV < obs_count[device]
    owner = obs_owner[:, 0]
    row_base = owner // N_TY * FX + obs_column // FY
    col_base = owner % N_TY * FY + obs_column % FY
    hx = jnp.zeros((NOBS,), jnp.float32)
    corners = []
    for offset_x in (0, 1):
        for offset_y in (0, 1):
            for offset_l in (0, 1):
                weight_x = obs_frac[0] if offset_x else 1.0 - obs_frac[0]
                weight_y = obs_frac[1] if offset_y else 1.0 - obs_frac[1]
                weight_l = obs_frac[2] if offset_l else 1.0 - obs_frac[2]
                weight = weight_x * weight_y * weight_l
                level = obs_level + offset_l
                across = row_base + offset_x
                along = col_base + offset_y
                hx = hx + weight * increment[level, across, along]
                corners.append((level, across, along, weight))
    departure = hx - innovation
    departures = jnp.where(live, departure, 0.0)
    weighted = jnp.where(live, obs_rinv * departure, 0.0)
    adjoint_grid_values = jnp.zeros((LEV, NFX, NFY), jnp.float32)
    for level, across, along, weight in corners:
        adjoint_grid_values = adjoint_grid_values.at[level, across, along].add(weighted * weight)
    grad_static = static_ctrl + bg_sigma * adjoint_grid_values

    def backward(running_total, member_perturbation):
        return (running_total, coarsen_field(member_perturbation.astype(jnp.float32) * adjoint_grid_values))
    unused, back = lax.scan(backward, jnp.float32(0.0), ens_pert)
    smooth_back = diffuse(jnp.moveaxis(back, 0, 2))
    mixed = jnp.einsum('xykl,lm->xykm', smooth_back, lv_sqrt, precision=highest)
    grad_alpha = alpha + mixed.reshape(NCX, NCY, MEMBERS * LEV)
    return (grad_alpha, grad_static, departures)
```

```python
import functools
import numpy as np
import jax
import jax.numpy as jnp
from jax import lax
from jax.experimental import pallas as pl
from jax.experimental.pallas import tpu as pltpu
from jax.sharding import PartitionSpec as P

F32 = jnp.float32
BF16 = jnp.bfloat16
NU = 0.2
RATIO = 4
VMEM_LIMIT = 56 * 1024 * 1024
NN = (((1,), (0,)), ((), ()))
NT = (((1,), (1,)), ((), ()))
TN = (((0,), (0,)), ((), ()))


def mm(a, b, dims=NN):
    return lax.dot_general(a, b, dims, preferred_element_type=F32)


def split(v):
    hi = v.astype(BF16)
    return hi, (v - hi.astype(F32)).astype(BF16)


def iota(shape, dim):
    return lax.broadcasted_iota(jnp.int32, shape, dim)


def route_kernel(cnt_ref, owner_ref, col_ref, lev_ref, frac_ref, inn_ref, rinv_ref, out_ref, tgt_ref, acc_ref):
    rows, wide = owner_ref.shape
    groups = 32
    place = iota((rows, wide), 0) * wide + iota((rows, wide), 1)
    live = place < cnt_ref[0]
    owner = jnp.where(live, owner_ref[...], groups)
    same = iota((rows, groups, wide), 1) == owner[:, None, :]
    onehot = jnp.where(same, 1.0, 0.0).astype(BF16).reshape(rows * groups, wide)
    before = jnp.where(iota((wide, wide), 0) < iota((wide, wide), 1), 1.0, 0.0).astype(BF16)
    inside = mm(onehot, before).reshape(rows, groups, wide)
    totals = mm(onehot, jnp.ones((wide, wide), BF16)).reshape(rows, groups, wide)
    running = jnp.zeros((groups, wide), F32)
    ranks = []
    for c in range(rows):
        ranks.append(jnp.sum(jnp.where(same[c], inside[c] + running, 0.0), 0, keepdims=True))
        running = running + totals[c]
    rank = jnp.concatenate(ranks, 0).astype(jnp.int32)
    low = rank % 128
    part = rank // 128
    tgt_ref[...] = jnp.where(live, owner * 512 + rank, -1)
    high = jnp.where(live, part * groups + owner, -1)
    base = (lev_ref[...] * 4096 + col_ref[...]).astype(F32)
    values = [frac_ref[0], frac_ref[1], frac_ref[2], inn_ref[...], rinv_ref[...], base]
    terms = []
    for v in values:
        terms.extend(split(v))
    acc_ref[...] = jnp.zeros_like(acc_ref)
    for c in range(rows):
        hit = jnp.where(iota((128, wide), 0) == high[c:c + 1], 1.0, 0.0).astype(BF16)
        lane = jnp.where(iota((128, wide), 0) == low[c:c + 1], 1.0, 0.0).astype(BF16)
        stack = jnp.concatenate([lane * t[c:c + 1] for t in terms], 0)
        acc_ref[...] += mm(hit, stack, NT)
    for ch in range(6):
        full = acc_ref[:, 256 * ch:256 * ch + 128] + acc_ref[:, 256 * ch + 128:256 * ch + 256]
        for q in range(4):
            out_ref[:, ch * 4 + q, :] = full[q * groups:(q + 1) * groups]


def route(cnt, owner, col, lev, frac, inn, rinv):
    slots = owner.shape[0]
    shape = (slots // 256, 256)
    return pl.pallas_call(
        route_kernel,
        out_shape=(jax.ShapeDtypeStruct((32, 24, 128), F32), jax.ShapeDtypeStruct(shape, jnp.int32)),
        in_specs=[pl.BlockSpec(memory_space=pltpu.SMEM)] + [pl.BlockSpec(memory_space=pltpu.VMEM)] * 6,
        out_specs=(pl.BlockSpec(memory_space=pltpu.VMEM),) * 2,
        scratch_shapes=[pltpu.VMEM((128, 1536), F32)],
        compiler_params=pltpu.CompilerParams(vmem_limit_bytes=VMEM_LIMIT),
        cost_estimate=pl.CostEstimate(flops=4_000_000_000, bytes_accessed=1_000_000, transcendentals=0),
        name="route",
    )(cnt, owner.reshape(shape), col.reshape(shape), lev.reshape(shape), frac.reshape((3,) + shape), inn.reshape(shape), rinv.reshape(shape))


def unroute_kernel(tgt_ref, ret_ref, out_ref):
    rows, wide = tgt_ref.shape
    ret = ret_ref[...].T
    hi, lo = split(ret)
    table = jnp.concatenate([hi, lo], 0)
    for c in range(rows):
        tgt = tgt_ref[c:c + 1]
        hit = jnp.where(iota((128, wide), 0) == tgt // 128, 1.0, 0.0).astype(BF16)
        picked = mm(table, hit)
        picked = picked[:128] + picked[128:]
        out_ref[c:c + 1] = jnp.sum(jnp.where((iota((128, wide), 0) == tgt % 128) & (tgt >= 0), picked, 0.0), 0, keepdims=True)


def unroute(tgt, ret):
    return pl.pallas_call(
        unroute_kernel,
        out_shape=jax.ShapeDtypeStruct(tgt.shape, F32),
        in_specs=[pl.BlockSpec(memory_space=pltpu.VMEM)] * 2,
        out_specs=pl.BlockSpec(memory_space=pltpu.VMEM),
        compiler_params=pltpu.CompilerParams(vmem_limit_bytes=VMEM_LIMIT),
        cost_estimate=pl.CostEstimate(flops=600_000_000, bytes_accessed=200_000, transcendentals=0),
        name="unroute",
    )(tgt, ret)


def tent(position, count):
    return jnp.maximum(1.0 - jnp.abs(position - iota((count, 128), 0).astype(F32)), 0.0)


def stencil_kernel(inc_ref, obs_ref, dep_ref, adj_ref, table_ref, acc_ref, ahi_ref, alo_ref):
    turned = inc_ref[...].T
    hi, lo = split(turned)
    table_ref[0:128] = hi
    table_ref[128:256] = lo
    acc_ref[...] = jnp.zeros_like(acc_ref)

    def one_source(s, carry):
        cols = []
        for q in range(4):
            get = lambda ch: obs_ref[s, ch * 4 + q:ch * 4 + q + 1, :]
            base = get(5).astype(jnp.int32)
            pos_l = (base // 4096).astype(F32) + get(2)
            pos_x = ((base // 128) % 32).astype(F32) + get(0)
            pos_y = (base % 128).astype(F32) + get(1)
            in_l, in_x = tent(pos_l, 32), tent(pos_x, 32)
            cols.append(tent(pos_y, 128))
            for l in range(32):
                hi, lo = split(in_l[l:l + 1] * in_x)
                ahi_ref[l * 32:(l + 1) * 32, q * 128:(q + 1) * 128] = hi
                alo_ref[l * 32:(l + 1) * 32, q * 128:(q + 1) * 128] = lo
        both = mm(table_ref[...], ahi_ref[...])
        picked = both[:128] + both[128:] + mm(table_ref[0:128], alo_ref[...])
        shi, slo = [], []
        for q in range(4):
            dep = jnp.sum(picked[:, q * 128:(q + 1) * 128] * cols[q], 0, keepdims=True) - obs_ref[s, 12 + q:13 + q, :]
            dep_ref[s, q:q + 1, :] = dep
            hi, lo = split(cols[q] * (dep * obs_ref[s, 16 + q:17 + q, :]))
            shi.append(hi)
            slo.append(lo)
        shi = jnp.concatenate(shi, 1)
        slo = jnp.concatenate(slo, 1)
        acc_ref[...] += mm(ahi_ref[...], shi, NT) + mm(ahi_ref[...], slo, NT) + mm(alo_ref[...], shi, NT)
        return carry

    lax.fori_loop(0, obs_ref.shape[0], one_source, 0)
    adj_ref[...] = acc_ref[...]


def stencil(inc, obs):
    return pl.pallas_call(
        stencil_kernel,
        out_shape=(jax.ShapeDtypeStruct((32, 4, 128), F32), jax.ShapeDtypeStruct((1024, 128), F32)),
        in_specs=[pl.BlockSpec(memory_space=pltpu.VMEM)] * 2,
        out_specs=(pl.BlockSpec(memory_space=pltpu.VMEM),) * 2,
        scratch_shapes=[
            pltpu.VMEM((256, 1024), BF16),
            pltpu.VMEM((1024, 128), F32),
            pltpu.VMEM((1024, 512), BF16),
            pltpu.VMEM((1024, 512), BF16),
        ],
        compiler_params=pltpu.CompilerParams(vmem_limit_bytes=VMEM_LIMIT),
        name="stencil",
    )(inc, obs)


def line_weights(fine, coarse):
    out = np.zeros((fine, coarse), np.float32)
    for f in range(fine):
        out[f, f // RATIO] += 1.0 - (f % RATIO) / RATIO
        out[f, f // RATIO + 1] += (f % RATIO) / RATIO
    return out


def tables():
    along = line_weights(128, 40)
    across = line_weights(32, 16)
    spread_y = np.concatenate([along.T, along.T], 0)
    gather_y = np.concatenate([along.T, along.T], 1)
    eye = np.eye(8, dtype=np.float32)
    block = np.kron(eye, across)
    spread_x = np.concatenate([block, block], 1)
    gather_x = np.concatenate([block.T, block.T], 1)
    return [jnp.asarray(t, BF16) for t in (spread_y, gather_y, spread_x, gather_x)]


def diffuse_rows(field, first, last):
    near = field[first - 1:last - 1] + field[first + 1:last + 1]
    mid = field[first:last]
    near = near + pltpu.roll(mid, 1, 1) + pltpu.roll(mid, 47, 1)
    return mid + NU * (near - 4.0 * mid)


def three(a, b_ref):
    hi, lo = split(a)
    return mm(jnp.concatenate([hi, lo, hi], 1), b_ref[...])


def forward_kernel(ext_ref, pert_ref, mix_ref, sy_ref, sx_ref, inc_ref, turn_ref):
    g = pl.program_id(0)

    @pl.when(g == 0)
    def _():
        inc_ref[...] = jnp.zeros_like(inc_ref)
        turn_ref[...] = jnp.zeros_like(turn_ref)

    field = ext_ref[...]
    for step in range(4):
        field = diffuse_rows(field, 1, field.shape[0] - 1)
    field = field[:, 8:48].reshape(9 * 40, 128)
    field = three(field, mix_ref).reshape(9, 40, 128)
    for a in range(9):
        hi, lo = split(field[a])
        turn_ref[:, a, :] = mm(jnp.concatenate([hi, lo], 0), sy_ref[...], TN)
    for i in range(16):
        hi, lo = split(turn_ref[8 * i:8 * i + 8].reshape(128, 128))
        fine = mm(sx_ref[...], jnp.concatenate([hi, lo], 0)).reshape(8, 32, 128)
        l0 = i % 4 * 8
        inc_ref[l0:l0 + 8] += fine * pert_ref[i // 4, l0:l0 + 8].astype(F32)


def forward(ext, pert, mix, sy, sx):
    whole = lambda a: pl.BlockSpec(a.shape, lambda g: (0,) * a.ndim)
    return pl.pallas_call(
        forward_kernel,
        grid=(5,),
        out_shape=jax.ShapeDtypeStruct((32, 32, 128), F32),
        in_specs=[
            pl.BlockSpec((17, 48, 128), lambda g: (0, 0, g)),
            pl.BlockSpec((4, 32, 32, 128), lambda g: (g, 0, 0, 0)),
            whole(mix), whole(sy), whole(sx),
        ],
        out_specs=pl.BlockSpec((32, 32, 128), lambda g: (0, 0, 0)),
        scratch_shapes=[pltpu.VMEM((128, 16, 128), F32)],
        compiler_params=pltpu.CompilerParams(vmem_limit_bytes=VMEM_LIMIT),
        name="forward",
    )(ext, pert, mix, sy, sx)


def backward_kernel(adj_ref, pert_ref, mix_ref, gy_ref, gx_ref, out_ref, turn_ref, grid_ref):
    for i in range(16):
        l0 = i % 4 * 8
        fine = adj_ref[l0:l0 + 8] * pert_ref[i // 4, l0:l0 + 8].astype(F32)
        hi, lo = split(fine.reshape(256, 128))
        turn_ref[8 * i:8 * i + 8] = mm(gx_ref[...], jnp.concatenate([hi, lo], 0)).reshape(8, 16, 128)
    rows = []
    for a in range(9):
        hi, lo = split(turn_ref[:, a, :])
        rows.append(mm(gy_ref[...], jnp.concatenate([hi, lo], 1), NT))
    field = three(jnp.concatenate(rows, 0), mix_ref).reshape(9, 40, 128)
    field = jnp.concatenate([jnp.zeros((9, 8, 128), F32), field], 1)
    for step in range(4):
        two = jnp.zeros((2, 48, 128), F32)
        field = jnp.concatenate([two, field, two], 0)
        field = diffuse_rows(field, 1, field.shape[0] - 1)
    out_ref[...] = field


def backward(adj, pert, mix, gy, gx):
    whole = lambda a: pl.BlockSpec(a.shape, lambda g: (0,) * a.ndim)
    return pl.pallas_call(
        backward_kernel,
        grid=(5,),
        out_shape=jax.ShapeDtypeStruct((17, 48, 640), F32),
        in_specs=[
            whole(adj),
            pl.BlockSpec((4, 32, 32, 128), lambda g: (g, 0, 0, 0)),
            whole(mix), whole(gy), whole(gx),
        ],
        out_specs=pl.BlockSpec((17, 48, 128), lambda g: (0, 0, g)),
        scratch_shapes=[pltpu.VMEM((128, 16, 128), F32), pltpu.VMEM((17, 48, 128), F32)],
        compiler_params=pltpu.CompilerParams(vmem_limit_bytes=VMEM_LIMIT),
        name="backward",
    )(adj, pert, mix, gy, gx)


def mixing(lv):
    eye = jnp.eye(4, dtype=F32)
    def stacked(m):
        hi, lo = split(jnp.kron(eye, m))
        return jnp.concatenate([hi, hi, lo], 0)
    return stacked(lv.T), stacked(lv)


def shifted(value, axis, by):
    count = lax.axis_size(axis)
    return lax.ppermute(value, axis, [(i, (i + by) % count) for i in range(count)])


def per_device(alpha, lv_sqrt, ens_pert, bg_sigma, static_ctrl, obs_owner, obs_column, obs_level, obs_frac, innovation, obs_rinv, obs_count):
    mix_forward, mix_backward = mixing(lv_sqrt)
    spread_y, gather_y, spread_x, gather_x = tables()
    above = shifted(alpha[4:], "tx", 1)
    below = shifted(alpha[:5], "tx", -1)
    outgoing, target = route(obs_count, obs_owner[:, 0], obs_column, obs_level, obs_frac, innovation, obs_rinv)
    incoming = lax.all_to_all(outgoing, ("tx", "ty"), split_axis=0, concat_axis=0, tiled=True)
    tall = jnp.concatenate([above, alpha, below], 0)
    left = shifted(tall[:, 24:], "ty", 1)
    right = shifted(tall[:, :8], "ty", -1)
    ext = jnp.concatenate([left, tall, right], 1)
    partial = forward(ext, ens_pert, mix_forward, spread_y, spread_x)
    increment = lax.psum(partial, "mem") + bg_sigma * static_ctrl
    departure, adjoint = stencil(increment.reshape(1024, 128), incoming)
    returned = lax.all_to_all(departure, ("tx", "ty"), split_axis=0, concat_axis=0, tiled=True)
    adjoint = lax.psum(adjoint, "mem").reshape(32, 32, 128)
    grad_static = static_ctrl + bg_sigma * adjoint
    back = backward(adjoint, ens_pert, mix_backward, gather_y, gather_x)
    departures = unroute(target, returned.reshape(128, 128)).reshape(-1)
    above = shifted(back[12:], "tx", 1)
    below = shifted(back[:4], "tx", -1)
    tall = back[4:12].at[:5].add(above).at[4:].add(below)
    left = shifted(tall[:, 40:45], "ty", 1)
    right = shifted(tall[:, 4:8], "ty", -1)
    center = tall[:, 8:40].at[:, :5].add(left).at[:, 28:].add(right)
    return alpha + center, grad_static, departures


def solution(mesh):
    placed = (
        P("tx", "ty", "mem"),
        P(),
        P("mem", None, "tx", "ty"),
        P(None, "tx", "ty"),
        P(None, "tx", "ty"),
        P(("tx", "ty", "mem"), None),
        P(("tx", "ty", "mem")),
        P(("tx", "ty", "mem")),
        P(None, ("tx", "ty", "mem")),
        P(("tx", "ty", "mem")),
        P(("tx", "ty", "mem")),
        P(("tx", "ty", "mem")),
    )
    return jax.shard_map(
        per_device,
        mesh=mesh,
        in_specs=placed,
        out_specs=(P("tx", "ty", "mem"), P(None, "tx", "ty"), P(("tx", "ty", "mem"))),
        check_vma=False,
    )
```

```python
import functools
import numpy as np
import jax
import jax.numpy as jnp
from jax import lax
from jax.experimental import pallas as pl
from jax.experimental.pallas import tpu as pltpu
from jax.sharding import PartitionSpec as P

F32 = jnp.float32
BF16 = jnp.bfloat16
NU = 0.2
RATIO = 4
VMEM_LIMIT = 56 * 1024 * 1024
NN = (((1,), (0,)), ((), ()))
NT = (((1,), (1,)), ((), ()))
TN = (((0,), (0,)), ((), ()))


def mm(a, b, dims=NN):
    return lax.dot_general(a, b, dims, preferred_element_type=F32)


def split(v):
    hi = v.astype(BF16)
    return hi, (v - hi.astype(F32)).astype(BF16)


def iota(shape, dim):
    return lax.broadcasted_iota(jnp.int32, shape, dim)


def tent(position, count):
    return jnp.maximum(1.0 - jnp.abs(position - iota((count, 128), 0).astype(F32)), 0.0)


def stencil_kernel(inc_ref, obs_ref, dep_ref, adj_ref, table_ref, acc_ref, ahi_ref, alo_ref):
    turned = inc_ref[...].T
    hi, lo = split(turned)
    table_ref[0:128] = hi
    table_ref[128:256] = lo
    acc_ref[...] = jnp.zeros_like(acc_ref)

    def one_source(s, carry):
        cols = []
        for q in range(4):
            get = lambda ch: obs_ref[s, ch * 4 + q:ch * 4 + q + 1, :]
            base = get(5).astype(jnp.int32)
            pos_l = (base // 4096).astype(F32) + get(2)
            pos_x = ((base // 128) % 32).astype(F32) + get(0)
            pos_y = (base % 128).astype(F32) + get(1)
            in_l, in_x = tent(pos_l, 32), tent(pos_x, 32)
            cols.append(tent(pos_y, 128))
            for l in range(32):
                hi, lo = split(in_l[l:l + 1] * in_x)
                ahi_ref[l * 32:(l + 1) * 32, q * 128:(q + 1) * 128] = hi
                alo_ref[l * 32:(l + 1) * 32, q * 128:(q + 1) * 128] = lo
        both = mm(table_ref[...], ahi_ref[...])
        picked = both[:128] + both[128:] + mm(table_ref[0:128], alo_ref[...])
        shi, slo = [], []
        for q in range(4):
            dep = jnp.sum(picked[:, q * 128:(q + 1) * 128] * cols[q], 0, keepdims=True) - obs_ref[s, 12 + q:13 + q, :]
            dep_ref[s, q:q + 1, :] = dep
            hi, lo = split(cols[q] * (dep * obs_ref[s, 16 + q:17 + q, :]))
            shi.append(hi)
            slo.append(lo)
        shi = jnp.concatenate(shi, 1)
        slo = jnp.concatenate(slo, 1)
        acc_ref[...] += mm(ahi_ref[...], shi, NT) + mm(ahi_ref[...], slo, NT) + mm(alo_ref[...], shi, NT)
        return carry

    lax.fori_loop(0, obs_ref.shape[0], one_source, 0)
    adj_ref[...] = acc_ref[...]


def stencil(inc, obs):
    return pl.pallas_call(
        stencil_kernel,
        out_shape=(jax.ShapeDtypeStruct((32, 4, 128), F32), jax.ShapeDtypeStruct((1024, 128), F32)),
        in_specs=[pl.BlockSpec(memory_space=pltpu.VMEM)] * 2,
        out_specs=(pl.BlockSpec(memory_space=pltpu.VMEM),) * 2,
        scratch_shapes=[
            pltpu.VMEM((256, 1024), BF16),
            pltpu.VMEM((1024, 128), F32),
            pltpu.VMEM((1024, 512), BF16),
            pltpu.VMEM((1024, 512), BF16),
        ],
        compiler_params=pltpu.CompilerParams(vmem_limit_bytes=VMEM_LIMIT),
        name="stencil",
    )(inc, obs)


def line_weights(fine, coarse):
    out = np.zeros((fine, coarse), np.float32)
    for f in range(fine):
        out[f, f // RATIO] += 1.0 - (f % RATIO) / RATIO
        out[f, f // RATIO + 1] += (f % RATIO) / RATIO
    return out


def tables():
    along = line_weights(128, 40)
    across = line_weights(32, 16)
    spread_y = np.concatenate([along.T, along.T], 0)
    gather_y = np.concatenate([along.T, along.T], 1)
    eye = np.eye(8, dtype=np.float32)
    block = np.kron(eye, across)
    spread_x = np.concatenate([block, block], 1)
    gather_x = np.concatenate([block.T, block.T], 1)
    return [jnp.asarray(t, BF16) for t in (spread_y, gather_y, spread_x, gather_x)]


def diffuse_rows(field, first, last):
    near = field[first - 1:last - 1] + field[first + 1:last + 1]
    mid = field[first:last]
    near = near + pltpu.roll(mid, 1, 1) + pltpu.roll(mid, 47, 1)
    return mid + NU * (near - 4.0 * mid)


def three(a, b_ref):
    hi, lo = split(a)
    return mm(jnp.concatenate([hi, lo, hi], 1), b_ref[...])

MESH = pl.DeviceIdType.MESH
GROUPS = 32
CHUNKS = 5
BLOCKS = 4


def tile_id(index, mem):
    return (index // 4, index % 4, mem)


def remote(src, dst, send, recv, device):
    return pltpu.make_async_remote_copy(src_ref=src, dst_ref=dst, send_sem=send, recv_sem=recv, device_id=device, device_id_type=MESH)


class Place:
    def __init__(self):
        self.tx, self.ty, self.mem = lax.axis_index("tx"), lax.axis_index("ty"), lax.axis_index("mem")
        self.tile = self.tx * 4 + self.ty
        self.core = self.mem % 2
        self.below = (lax.rem(self.tx + 1, 8), self.ty, self.mem)
        self.above = (lax.rem(self.tx + 7, 8), self.ty, self.mem)
        self.right = (self.tx, lax.rem(self.ty + 1, 4), self.mem)
        self.left = (self.tx, lax.rem(self.ty + 3, 4), self.mem)
        self.twin = (self.tx, self.ty, self.mem + 1 - 2 * self.core)
        self.across = (self.tx, self.ty, lax.rem(self.mem + 2, 4))

    def greet(self):
        barrier = pltpu.get_barrier_semaphore()

        def one(d, carry):
            other = lax.rem(self.tile + d, GROUPS)
            pl.semaphore_signal(barrier, inc=1, device_id=tile_id(other, self.mem), device_id_type=MESH)
            return carry

        lax.fori_loop(1, GROUPS, one, 0)
        for other in (self.twin, self.across):
            pl.semaphore_signal(barrier, inc=1, device_id=other, device_id_type=MESH)
        pl.semaphore_wait(barrier, GROUPS + 1)


class Exchange:
    def __init__(self, place, src, dst, send, recv, own):
        self.place, self.src, self.dst, self.send, self.recv = place, src, dst, send, recv
        self.own = pltpu.make_async_copy(src.at[place.tile], dst.at[place.tile], own)

    def copy(self, d):
        other = lax.rem(self.place.tile + d, GROUPS)
        return remote(self.src.at[other], self.dst.at[self.place.tile], self.send.at[d], self.recv.at[d], tile_id(other, self.place.mem))

    def start(self):
        self.own.start()

        def one(d, carry):
            self.copy(d).start()
            return carry

        lax.fori_loop(1, GROUPS, one, 0)

    def wait(self):
        self.own.wait()

        def one(d, carry):
            self.copy(d).wait()
            return carry

        lax.fori_loop(1, GROUPS, one, 0)


class MemSum:
    def __init__(self, place, part, total, half, got, far, send, recv):
        self.place, self.part, self.total = place, part, total
        self.half, self.got, self.far, self.send, self.recv = half, got, far, send, recv

    def mine(self, b):
        return pl.ds(8 * b + 4 * self.place.core, 4)

    def near(self, b):
        return remote(self.part.at[pl.ds(8 * b + 4 - 4 * self.place.core, 4)], self.got.at[b], self.send.at[0, b], self.recv.at[0, b], self.place.twin)

    def over(self, b):
        return remote(self.half.at[b], self.far.at[b], self.send.at[1, b], self.recv.at[1, b], self.place.across)

    def back(self, b):
        return remote(self.total.at[self.mine(b)], self.total.at[self.mine(b)], self.send.at[2, b], self.recv.at[2, b], self.place.twin)

    def second(self, b):
        self.near(b).wait()
        self.half[b] = self.part[self.mine(b)] + self.got[b]
        self.over(b).start()

    def third(self, b, extra):
        self.over(b).wait()
        self.total[self.mine(b)] = self.half[b] + self.far[b] + extra(self.mine(b))
        self.back(b).start()

    def last(self, b):
        self.back(b).wait()


MEM_SCRATCH = [pltpu.VMEM((BLOCKS, 4, 32, 128), F32)] * 3 + [pltpu.SemaphoreType.DMA((3, BLOCKS))] * 2


def route_ranks(cnt_ref, owner_ref, col_ref, lev_ref, frac_ref, inn_ref, rinv_ref, tgt_ref, high_ref, low_ref, term_ref):
    rows, wide = owner_ref.shape
    place = iota((rows, wide), 0) * wide + iota((rows, wide), 1)
    live = place < cnt_ref[0]
    owner = jnp.where(live, owner_ref[...], GROUPS)
    same = iota((rows, GROUPS, wide), 1) == owner[:, None, :]
    onehot = jnp.where(same, 1.0, 0.0).astype(BF16).reshape(rows * GROUPS, wide)
    lower = iota((wide, 2 * wide), 0) < iota((wide, 2 * wide), 1)
    both = mm(onehot, jnp.where(lower, 1.0, 0.0).astype(BF16))
    inside, totals = both[:, :wide].reshape(rows, GROUPS, wide), both[:, wide:].reshape(rows, GROUPS, wide)
    running = jnp.zeros((GROUPS, wide), F32)
    ranks = []
    for c in range(rows):
        ranks.append(jnp.sum(jnp.where(same[c], inside[c] + running, 0.0), 0, keepdims=True))
        running = running + totals[c]
    rank = jnp.concatenate(ranks, 0).astype(jnp.int32)
    tgt_ref[...] = jnp.where(live, owner * 512 + rank, -1)
    high_ref[...] = jnp.where(live, rank // 128 * GROUPS + owner, -1)
    low_ref[...] = rank % 128
    base = (lev_ref[...] * 4096 + col_ref[...]).astype(F32)
    for at, v in ((3, inn_ref[...]), (4, rinv_ref[...]), (5, base)):
        hi, lo = split(v)
        term_ref[2 * at] = hi.astype(F32)
        term_ref[2 * at + 1] = lo.astype(F32)
    for at in range(3):
        for r in range(rows):
            hi, lo = split(frac_ref[at:at + 1, wide * r:wide * (r + 1)])
            term_ref[2 * at, r:r + 1] = hi.astype(F32)
            term_ref[2 * at + 1, r:r + 1] = lo.astype(F32)


def route_slots(high_ref, low_ref, term_ref, acc_ref, out_ref):
    acc_ref[...] = jnp.zeros_like(acc_ref)

    def one(c, carry):
        def pair(ref, *at):
            r = 2 * c
            return jnp.concatenate([ref[(*at, pl.ds(r, 1), slice(None))], ref[(*at, pl.ds(r + 1, 1), slice(None))]], 1)

        hit = jnp.where(iota((128, 256), 0) == pair(high_ref), 1.0, 0.0).astype(BF16)
        lane = jnp.where(iota((128, 256), 0) == pair(low_ref), 1.0, 0.0).astype(BF16)
        stack = jnp.concatenate([lane * pair(term_ref, t).astype(BF16) for t in range(12)], 0)
        acc_ref[...] += mm(hit, stack, NT)
        return carry

    lax.fori_loop(0, 32, one, 0, unroll=2)
    for ch in range(6):
        full = acc_ref[:, 256 * ch:256 * ch + 128] + acc_ref[:, 256 * ch + 128:256 * ch + 256]
        for q in range(4):
            out_ref[:, ch * 4 + q, :] = full[q * GROUPS:(q + 1) * GROUPS]


def unroute(tgt_ref, ret, out_ref):
    rows = tgt_ref.shape[0]
    hi, lo = split(ret.T)
    table = jnp.concatenate([hi, lo], 0)
    for c in range(0, rows, 2):
        tgt = jnp.concatenate([tgt_ref[c:c + 1], tgt_ref[c + 1:c + 2]], 1)
        hit = jnp.where(iota((128, 256), 0) == tgt // 128, 1.0, 0.0).astype(BF16)
        picked = mm(table, hit)
        picked = picked[:128] + picked[128:]
        row = jnp.sum(jnp.where((iota((128, 256), 0) == tgt % 128) & (tgt >= 0), picked, 0.0), 0, keepdims=True)
        out_ref[c:c + 1] = row[:, :128]
        out_ref[c + 1:c + 2] = row[:, 128:]


def diffuse_rows(field):
    near = field[:-2] + field[2:]
    mid = field[1:-1]
    near = near + pltpu.roll(mid, 1, 1) + pltpu.roll(mid, 47, 1)
    return mid + NU * (near - 4.0 * mid)


def three(a, b):
    hi, lo = split(a)
    bhi, blo = split(b)
    return mm(jnp.concatenate([hi, lo, hi], 1), jnp.concatenate([bhi, bhi, blo], 0))


def forward_kernel(
    cnt_ref, owner_ref, col_ref, lev_ref, frac_ref, inn_ref, rinv_ref, alpha_ref, pert_hbm, bg_ref, static_ref, mix_ref, sy_ref, sx_ref,
    inc_ref, obs_ref, tgt_ref,
    ext_ref, pert_ref, turn_ref, part_ref, out_ref, high_ref, low_ref, term_ref, acc_ref,
    half_ref, got_ref, far_ref, msend, mrecv,
    xsend, xrecv, ysend, yrecv, osend, orecv, own,
):
    place = Place()

    def x_copies(g):
        lanes = pl.ds(pl.multiple_of(g * 128, 128), 128)
        return (
            remote(alpha_ref.at[4:8, :, lanes], ext_ref.at[g, 0:4, 8:40], xsend.at[0, g], xrecv.at[0, g], place.below),
            remote(alpha_ref.at[0:5, :, lanes], ext_ref.at[g, 12:17, 8:40], xsend.at[1, g], xrecv.at[1, g], place.above),
        )

    def y_copies(g):
        return (
            remote(ext_ref.at[g, :, 32:40], ext_ref.at[g, :, 0:8], ysend.at[0, g], yrecv.at[0, g], place.right),
            remote(ext_ref.at[g, :, 8:16], ext_ref.at[g, :, 40:48], ysend.at[1, g], yrecv.at[1, g], place.left),
        )

    def own_copy(g):
        lanes = pl.ds(pl.multiple_of(g * 128, 128), 128)
        return pltpu.make_async_copy(alpha_ref.at[:, :, lanes], ext_ref.at[g, 4:12, 8:40], own.at[g])

    pert_copy = pltpu.make_async_copy(pert_hbm, pert_ref, own.at[CHUNKS])
    exchange = Exchange(place, out_ref, obs_ref, osend, orecv, own.at[CHUNKS + 1])
    total = MemSum(place, part_ref, inc_ref, half_ref, got_ref, far_ref, msend, mrecv)

    place.greet()

    def begin(g, carry):
        for copy in x_copies(g):
            copy.start()
        own_copy(g).start()
        return carry

    lax.fori_loop(0, CHUNKS, begin, 0)
    pert_copy.start()
    turn_ref[...] = jnp.zeros_like(turn_ref)
    route_ranks(cnt_ref, owner_ref, col_ref, lev_ref, frac_ref, inn_ref, rinv_ref, tgt_ref, high_ref, low_ref, term_ref)
    route_slots(high_ref, low_ref, term_ref, acc_ref, out_ref)

    def sideways(g, carry):
        for copy in x_copies(g):
            copy.wait()
        own_copy(g).wait()
        for copy in y_copies(g):
            copy.start()
        return carry

    lax.fori_loop(0, CHUNKS, sideways, 0)
    exchange.start()

    def smooth(g, carry):
        for copy in y_copies(g):
            copy.wait()
        field = ext_ref[g]
        for step in range(4):
            field = diffuse_rows(field)
        field = three(field[:, 8:48].reshape(9 * 40, 128), mix_ref[...]).reshape(9, 40, 128)
        for a in range(9):
            hi, lo = split(field[a])
            turn_ref[pl.ds(pl.multiple_of(g * 128, 128), 128), a, :] = mm(jnp.concatenate([hi, lo], 0), sy_ref[...], TN)
        return carry

    lax.fori_loop(0, CHUNKS, smooth, 0)
    pert_copy.wait()

    def block(b):
        def member(k, carry):
            hi, lo = split(turn_ref[pl.ds(k * 32 + 8 * b, 8)].reshape(128, 128))
            fine = mm(sx_ref[...], jnp.concatenate([hi, lo], 0)).reshape(8, 32, 128)
            return carry + fine * pert_ref[k, 8 * b:8 * b + 8].astype(F32)

        part_ref[8 * b:8 * b + 8] = lax.fori_loop(0, 20, member, jnp.zeros((8, 32, 128), F32), unroll=4)

    extra = lambda at: bg_ref[at] * static_ref[at]
    for s in range(BLOCKS + 3):
        if s < BLOCKS:
            block(s)
            total.near(s).start()
        if 0 <= s - 1 < BLOCKS:
            total.second(s - 1)
        if 0 <= s - 2 < BLOCKS:
            total.third(s - 2, extra)
        if 0 <= s - 3 < BLOCKS:
            total.last(s - 3)
    exchange.wait()


VMEM = pl.BlockSpec(memory_space=pltpu.VMEM)
SMEM = pl.BlockSpec(memory_space=pltpu.SMEM)
ANY = pl.BlockSpec(memory_space=pl.ANY)
DMA = pltpu.SemaphoreType.DMA


def forward(cnt, owner, col, lev, frac, inn, rinv, alpha, pert, bg, static, mix, sy, sx):
    return pl.pallas_call(
        forward_kernel,
        out_shape=(
            jax.ShapeDtypeStruct((32, 32, 128), F32),
            jax.ShapeDtypeStruct((GROUPS, 24, 128), F32),
            jax.ShapeDtypeStruct((64, 128), jnp.int32),
        ),
        in_specs=[SMEM] + [VMEM] * 6 + [ANY] * 2 + [VMEM] * 5,
        out_specs=(VMEM, VMEM, VMEM),
        scratch_shapes=[
            pltpu.VMEM((CHUNKS, 17, 48, 128), F32),
            pltpu.VMEM(pert.shape, BF16),
            pltpu.VMEM((640, 16, 128), F32),
            pltpu.VMEM((32, 32, 128), F32),
            pltpu.VMEM((GROUPS, 24, 128), F32),
            pltpu.VMEM((64, 128), jnp.int32),
            pltpu.VMEM((64, 128), jnp.int32),
            pltpu.VMEM((12, 64, 128), F32),
            pltpu.VMEM((128, 1536), F32),
        ] + MEM_SCRATCH + [DMA((2, CHUNKS))] * 4 + [DMA((GROUPS,))] * 2 + [DMA((CHUNKS + 2,))],
        compiler_params=pltpu.CompilerParams(vmem_limit_bytes=VMEM_LIMIT, collective_id=0, has_side_effects=True),
        name="forward",
    )(cnt, owner, col, lev, frac, inn, rinv, alpha, pert, bg, static, mix, sy, sx)


def backward_kernel(
    adj_ref, dep_ref, tgt_ref, alpha_ref, pert_hbm, bg_ref, static_ref, mix_ref, gy_ref, gx_ref,
    grad_ref, gstat_ref, depout_ref,
    full_ref, pert_ref, turn_ref, wide_ref, fromleft_ref, fromright_ref, fromabove_ref, frombelow_ref, ret_ref,
    half_ref, got_ref, far_ref, msend, mrecv,
    xsend, xrecv, ysend, yrecv, osend, orecv, own,
):
    place = Place()

    def y_copies(g):
        return (
            remote(wide_ref.at[g, :, 40:48], fromleft_ref.at[g], ysend.at[0, g], yrecv.at[0, g], place.right),
            remote(wide_ref.at[g, :, 0:8], fromright_ref.at[g], ysend.at[1, g], yrecv.at[1, g], place.left),
        )

    def x_copies(g):
        return (
            remote(wide_ref.at[g, 12:17, 8:40], fromabove_ref.at[g], xsend.at[0, g], xrecv.at[0, g], place.below),
            remote(wide_ref.at[g, 0:4, 8:40], frombelow_ref.at[g], xsend.at[1, g], xrecv.at[1, g], place.above),
        )

    pert_copy = pltpu.make_async_copy(pert_hbm, pert_ref, own.at[0])
    exchange = Exchange(place, dep_ref, ret_ref, osend, orecv, own.at[1])
    total = MemSum(place, adj_ref, full_ref, half_ref, got_ref, far_ref, msend, mrecv)

    place.greet()
    for b in range(BLOCKS):
        total.near(b).start()
    pert_copy.start()
    for b in range(BLOCKS):
        total.second(b)
    exchange.start()
    pert_copy.wait()

    def block(b):
        fine_adj = full_ref[8 * b:8 * b + 8]

        def member(k, carry):
            fine = fine_adj * pert_ref[k, 8 * b:8 * b + 8].astype(F32)
            hi, lo = split(fine.reshape(256, 128))
            turn_ref[pl.ds(k * 32 + 8 * b, 8)] = mm(gx_ref[...], jnp.concatenate([hi, lo], 0)).reshape(8, 16, 128)
            return carry

        lax.fori_loop(0, 20, member, 0, unroll=4)
        gstat_ref[8 * b:8 * b + 8] = static_ref[8 * b:8 * b + 8] + bg_ref[8 * b:8 * b + 8] * fine_adj

    for s in range(BLOCKS + 1):
        if s < BLOCKS:
            total.third(s, lambda at: 0.0)
        if s >= 1:
            total.last(s - 1)
            block(s - 1)

    def smooth(g, carry):
        rows = []
        for a in range(9):
            hi, lo = split(turn_ref[pl.ds(pl.multiple_of(g * 128, 128), 128), a, :])
            rows.append(mm(gy_ref[...], jnp.concatenate([hi, lo], 1), NT))
        field = three(jnp.concatenate(rows, 0), mix_ref[...]).reshape(9, 40, 128)
        field = jnp.concatenate([jnp.zeros((9, 8, 128), F32), field], 1)
        for step in range(4):
            two = jnp.zeros((2, 48, 128), F32)
            field = diffuse_rows(jnp.concatenate([two, field, two], 0))
        wide_ref[g] = field
        for copy in y_copies(g):
            copy.start()
        return carry

    def lengthways(g, carry):
        for copy in y_copies(g):
            copy.wait()
        wide_ref[g, :, 8:16] += fromleft_ref[g]
        wide_ref[g, :, 32:40] += fromright_ref[g]
        for copy in x_copies(g):
            copy.start()
        return carry

    def both(g, carry):
        smooth(g, carry)
        return lengthways(g - 1, carry)

    smooth(0, 0)
    lax.fori_loop(1, CHUNKS, both, 0)
    lengthways(CHUNKS - 1, 0)

    exchange.wait()
    unroute(tgt_ref, ret_ref[...].reshape(128, 128), depout_ref)
    for g in range(CHUNKS):
        for copy in x_copies(g):
            copy.wait()
        lanes = slice(128 * g, 128 * g + 128)
        grad_ref[:, :, lanes] = alpha_ref[:, :, lanes] + wide_ref[g, 4:12, 8:40]
        grad_ref[0:5, :, lanes] += fromabove_ref[g]
        grad_ref[4:8, :, lanes] += frombelow_ref[g]


def backward(adj, dep, tgt, alpha, pert, bg, static, mix, gy, gx):
    return pl.pallas_call(
        backward_kernel,
        out_shape=(
            jax.ShapeDtypeStruct(alpha.shape, F32),
            jax.ShapeDtypeStruct(static.shape, F32),
            jax.ShapeDtypeStruct(tgt.shape, F32),
        ),
        in_specs=[VMEM] * 4 + [ANY] + [VMEM] * 5,
        out_specs=(VMEM,) * 3,
        scratch_shapes=[
            pltpu.VMEM((32, 32, 128), F32),
            pltpu.VMEM(pert.shape, BF16),
            pltpu.VMEM((640, 16, 128), F32),
            pltpu.VMEM((CHUNKS, 17, 48, 128), F32),
            pltpu.VMEM((CHUNKS, 17, 8, 128), F32),
            pltpu.VMEM((CHUNKS, 17, 8, 128), F32),
            pltpu.VMEM((CHUNKS, 5, 32, 128), F32),
            pltpu.VMEM((CHUNKS, 4, 32, 128), F32),
            pltpu.VMEM((GROUPS, 4, 128), F32),
        ] + MEM_SCRATCH + [DMA((2, CHUNKS))] * 4 + [DMA((GROUPS,))] * 2 + [DMA((2,))],
        compiler_params=pltpu.CompilerParams(vmem_limit_bytes=VMEM_LIMIT, collective_id=1, has_side_effects=True),
        name="backward",
    )(adj, dep, tgt, alpha, pert, bg, static, mix, gy, gx)


def per_device(alpha, lv_sqrt, ens_pert, bg_sigma, static_ctrl, obs_owner, obs_column, obs_level, obs_frac, innovation, obs_rinv, obs_count):
    four = jnp.eye(4, dtype=F32)
    mix_forward, mix_backward = jnp.kron(four, lv_sqrt.T), jnp.kron(four, lv_sqrt)
    spread_y, gather_y, spread_x, gather_x = tables()
    shape = (64, 128)
    increment, incoming, target = forward(
        obs_count, obs_owner.reshape(shape), obs_column.reshape(shape), obs_level.reshape(shape), obs_frac,
        innovation.reshape(shape), obs_rinv.reshape(shape), alpha, ens_pert, bg_sigma, static_ctrl, mix_forward, spread_y, spread_x,
    )
    departure, adjoint = stencil(increment.reshape(1024, 128), incoming)
    grad_alpha, grad_static, departures = backward(
        adjoint.reshape(32, 32, 128), departure, target, alpha, ens_pert, bg_sigma, static_ctrl, mix_backward, gather_y, gather_x,
    )
    return grad_alpha, grad_static, departures.reshape(-1)


def solution(mesh):
    placed = (
        P("tx", "ty", "mem"),
        P(),
        P("mem", None, "tx", "ty"),
        P(None, "tx", "ty"),
        P(None, "tx", "ty"),
        P(("tx", "ty", "mem"), None),
        P(("tx", "ty", "mem")),
        P(("tx", "ty", "mem")),
        P(None, ("tx", "ty", "mem")),
        P(("tx", "ty", "mem")),
        P(("tx", "ty", "mem")),
        P(("tx", "ty", "mem")),
    )
    return jax.shard_map(
        per_device,
        mesh=mesh,
        in_specs=placed,
        out_specs=(P("tx", "ty", "mem"), P(None, "tx", "ty"), P(("tx", "ty", "mem"))),
        check_vma=False,
    )
```

```python
import functools
import numpy as np
import jax
import jax.numpy as jnp
from jax import lax
from jax.experimental import pallas as pl
from jax.experimental.pallas import tpu as pltpu
from jax.sharding import PartitionSpec as P

F32 = jnp.float32
BF16 = jnp.bfloat16
NU = 0.2
RATIO = 4
VMEM_LIMIT = 56 * 1024 * 1024
NN = (((1,), (0,)), ((), ()))
NT = (((1,), (1,)), ((), ()))
TN = (((0,), (0,)), ((), ()))


def mm(a, b, dims=NN):
    return lax.dot_general(a, b, dims, preferred_element_type=F32)


def split(v):
    hi = v.astype(BF16)
    return hi, (v - hi.astype(F32)).astype(BF16)


def iota(shape, dim):
    return lax.broadcasted_iota(jnp.int32, shape, dim)


def tent(position, count):
    return jnp.maximum(1.0 - jnp.abs(position - iota((count, 128), 0).astype(F32)), 0.0)


def chunk_order(obs_ref):
    base = obs_ref[:, 20:24, :].astype(jnp.int32)
    live = obs_ref[:, 16:20, :] > 0.0
    level = base // 4096
    first = jnp.min(jnp.where(live, level, 99), 2, keepdims=True).astype(F32)
    last = jnp.max(jnp.where(live, level + 1, -1), 2, keepdims=True).astype(F32)
    spread = lambda v: jnp.broadcast_to(v, (32, 4, 128)).reshape(128, 128)
    first, last = spread(first), spread(last)
    down, along = iota((128, 128), 0), iota((128, 128), 1)
    key = first * 16384.0 + last * 128.0 + down.astype(F32)
    other = key.T
    rank = jnp.sum(jnp.where(other > key, 1.0, 0.0), 0, keepdims=True)
    hit = along == jnp.broadcast_to(rank, (128, 128)).T.astype(jnp.int32)
    pick = lambda v: jnp.sum(jnp.where(hit, v, 0.0), 0, keepdims=True)
    live_count = jnp.sum(jnp.where(other < 99.0 * 16384.0, 1.0, 0.0), 1, keepdims=True)
    count = jnp.broadcast_to(live_count, (128, 128))[0:1]
    rows = [pick(down.astype(F32)), pick(first), pick(last), count]
    return jnp.concatenate(rows + [jnp.zeros((4, 128), F32)], 0).astype(jnp.int32)


def stencil_kernel(order_ref, table_ref, obs_ref, dep_ref, adj_ref, acc_ref, ahi_ref, alo_ref, in_l_ref, in_x_ref, in_y_ref, sum_ref, spread_ref):
    acc_ref[...] = jnp.zeros_like(acc_ref)
    dep_ref[...] = jnp.zeros_like(dep_ref)

    def blocks_of(n):
        first = jnp.int32(99)
        last = jnp.int32(-1)
        for j in range(4):
            first = jnp.minimum(first, order_ref[1, 4 * n + j])
            last = jnp.maximum(last, order_ref[2, 4 * n + j])
        return jnp.where(last < 0, 0, first // 8), jnp.where(last < 0, 0, last // 8 + 1)

    def adjoint(slot, g):
        acc_ref[g, 0:256] += mm(spread_ref[...], ahi_ref[slot, g], NT)
        acc_ref[g, 256:384] += mm(spread_ref[0:128], alo_ref[slot, g], NT)

    def one_group(n, before):
        slot = lax.rem(n, 2)
        old_from, old_to = before
        new_from, new_to = blocks_of(n)
        sources, parts = [], []
        for j in range(4):
            chunk = order_ref[0, 4 * n + j]
            s, q = chunk // 4, lax.rem(chunk, 4)
            sources.append(s)
            parts.append(q)
            get = lambda ch: obs_ref[s, pl.ds(ch * 4 + q, 1), :]
            base = get(5).astype(jnp.int32)
            at = slice(128 * j, 128 * j + 128)
            in_l_ref[:, at] = tent((base // 4096).astype(F32) + get(2), 32)
            in_x_ref[:, at] = tent(((base // 128) % 32).astype(F32) + get(0), 32)
            in_y_ref[:, at] = tent((base % 128).astype(F32) + get(1), 128)
        sum_ref[...] = jnp.zeros_like(sum_ref)

        def gather(g):
            in_l = in_l_ref[pl.ds(pl.multiple_of(8 * g, 8), 8), :]
            for l in range(8):
                hi, lo = split(in_l[l:l + 1] * in_x_ref[...])
                ahi_ref[slot, g, 32 * l:32 * l + 32] = hi
                alo_ref[slot, g, 32 * l:32 * l + 32] = lo
            both = mm(table_ref[g], ahi_ref[slot, g])
            sum_ref[...] += both[:128] + both[128:] + mm(table_ref[g, 0:128], alo_ref[slot, g])

        shared_from = jnp.maximum(old_from, new_from)
        shared_to = jnp.maximum(jnp.minimum(old_to, new_to), shared_from)

        def together(g, carry):
            adjoint(1 - slot, g)
            gather(g)
            return carry

        def only_old(g, carry):
            adjoint(1 - slot, g)
            return carry

        def only_new(g, carry):
            gather(g)
            return carry

        lax.fori_loop(old_from, jnp.minimum(old_to, shared_from), only_old, 0)
        lax.fori_loop(shared_to, old_to, only_old, 0)
        lax.fori_loop(shared_from, shared_to, together, 0)
        lax.fori_loop(new_from, jnp.minimum(new_to, shared_from), only_new, 0)
        lax.fori_loop(shared_to, new_to, only_new, 0)

        for j in range(4):
            at = slice(128 * j, 128 * j + 128)
            get = lambda ch: obs_ref[sources[j], pl.ds(ch * 4 + parts[j], 1), :]
            dep = jnp.sum(sum_ref[:, at] * in_y_ref[:, at], 0, keepdims=True) - get(3)
            dep_ref[sources[j], pl.ds(parts[j], 1), :] = dep
            hi, lo = split(in_y_ref[:, at] * (dep * get(4)))
            spread_ref[0:128, at] = hi
            spread_ref[128:256, at] = lo
        return new_from, new_to

    groups = (order_ref[3, 0] + 3) // 4
    old_from, old_to = lax.fori_loop(0, groups, one_group, (jnp.int32(0), jnp.int32(0)))

    def finish(g, carry):
        adjoint(lax.rem(groups + 1, 2), g)
        return carry

    lax.fori_loop(old_from, old_to, finish, 0)
    for g in range(4):
        adj_ref[256 * g:256 * g + 256] = (acc_ref[g, 0:128] + acc_ref[g, 128:256] + acc_ref[g, 256:384]).T


def stencil(order, table, obs):
    return pl.pallas_call(
        stencil_kernel,
        out_shape=(jax.ShapeDtypeStruct((32, 4, 128), F32), jax.ShapeDtypeStruct((1024, 128), F32)),
        in_specs=[pl.BlockSpec(memory_space=pltpu.SMEM)] + [pl.BlockSpec(memory_space=pltpu.VMEM)] * 2,
        out_specs=(pl.BlockSpec(memory_space=pltpu.VMEM),) * 2,
        scratch_shapes=[
            pltpu.VMEM((4, 384, 256), F32),
            pltpu.VMEM((2, 4, 256, 512), BF16),
            pltpu.VMEM((2, 4, 256, 512), BF16),
            pltpu.VMEM((32, 512), F32),
            pltpu.VMEM((32, 512), F32),
            pltpu.VMEM((128, 512), F32),
            pltpu.VMEM((128, 512), F32),
            pltpu.VMEM((256, 512), BF16),
        ],
        compiler_params=pltpu.CompilerParams(vmem_limit_bytes=VMEM_LIMIT),
        name="stencil",
    )(order, table, obs)


def line_weights(fine, coarse):
    out = np.zeros((fine, coarse), np.float32)
    for f in range(fine):
        out[f, f // RATIO] += 1.0 - (f % RATIO) / RATIO
        out[f, f // RATIO + 1] += (f % RATIO) / RATIO
    return out


def tables():
    along = line_weights(128, 40)
    across = line_weights(32, 16)
    spread_y = np.concatenate([along.T, along.T], 0)
    gather_y = np.concatenate([along.T, along.T], 1)
    eye = np.eye(8, dtype=np.float32)
    block = np.kron(eye, across)
    spread_x = np.concatenate([block, block], 1)
    gather_x = np.concatenate([block.T, block.T], 1)
    return [jnp.asarray(t, BF16) for t in (spread_y, gather_y, spread_x, gather_x)]


def diffuse_rows(field, first, last):
    near = field[first - 1:last - 1] + field[first + 1:last + 1]
    mid = field[first:last]
    near = near + pltpu.roll(mid, 1, 1) + pltpu.roll(mid, 47, 1)
    return mid + NU * (near - 4.0 * mid)


def three(a, b_ref):
    hi, lo = split(a)
    return mm(jnp.concatenate([hi, lo, hi], 1), b_ref[...])

MESH = pl.DeviceIdType.MESH
GROUPS = 32
CHUNKS = 5
BLOCKS = 4


def tile_id(index, mem):
    return (index // 4, index % 4, mem)


def remote(src, dst, send, recv, device):
    return pltpu.make_async_remote_copy(src_ref=src, dst_ref=dst, send_sem=send, recv_sem=recv, device_id=device, device_id_type=MESH)


class Place:
    def __init__(self):
        self.tx, self.ty, self.mem = lax.axis_index("tx"), lax.axis_index("ty"), lax.axis_index("mem")
        self.tile = self.tx * 4 + self.ty
        self.core = self.mem % 2
        self.below = (lax.rem(self.tx + 1, 8), self.ty, self.mem)
        self.above = (lax.rem(self.tx + 7, 8), self.ty, self.mem)
        self.right = (self.tx, lax.rem(self.ty + 1, 4), self.mem)
        self.left = (self.tx, lax.rem(self.ty + 3, 4), self.mem)
        self.twin = (self.tx, self.ty, self.mem + 1 - 2 * self.core)
        self.across = (self.tx, self.ty, lax.rem(self.mem + 2, 4))

    def greet(self):
        barrier = pltpu.get_barrier_semaphore()

        def one(d, carry):
            other = lax.rem(self.tile + d, GROUPS)
            pl.semaphore_signal(barrier, inc=1, device_id=tile_id(other, self.mem), device_id_type=MESH)
            return carry

        lax.fori_loop(1, GROUPS, one, 0)
        for other in (self.twin, self.across):
            pl.semaphore_signal(barrier, inc=1, device_id=other, device_id_type=MESH)
        pl.semaphore_wait(barrier, GROUPS + 1)


class Exchange:
    def __init__(self, place, src, dst, send, recv, own):
        self.place, self.src, self.dst, self.send, self.recv = place, src, dst, send, recv
        self.own = pltpu.make_async_copy(src.at[place.tile], dst.at[place.tile], own)

    def copy(self, d):
        other = lax.rem(self.place.tile + d, GROUPS)
        return remote(self.src.at[other], self.dst.at[self.place.tile], self.send.at[d], self.recv.at[d], tile_id(other, self.place.mem))

    def start(self):
        self.own.start()

        def one(d, carry):
            self.copy(d).start()
            return carry

        lax.fori_loop(1, GROUPS, one, 0)

    def wait(self):
        self.own.wait()

        def one(d, carry):
            self.copy(d).wait()
            return carry

        lax.fori_loop(1, GROUPS, one, 0)


class MemSum:
    def __init__(self, place, part, total, half, got, far, send, recv):
        self.place, self.part, self.total = place, part, total
        self.half, self.got, self.far, self.send, self.recv = half, got, far, send, recv

    def mine(self, b):
        return pl.ds(8 * b + 4 * self.place.core, 4)

    def near(self, b):
        return remote(self.part.at[pl.ds(8 * b + 4 - 4 * self.place.core, 4)], self.got.at[b], self.send.at[0, b], self.recv.at[0, b], self.place.twin)

    def over(self, b):
        return remote(self.half.at[b], self.far.at[b], self.send.at[1, b], self.recv.at[1, b], self.place.across)

    def back(self, b):
        return remote(self.total.at[self.mine(b)], self.total.at[self.mine(b)], self.send.at[2, b], self.recv.at[2, b], self.place.twin)

    def second(self, b):
        self.near(b).wait()
        self.half[b] = self.part[self.mine(b)] + self.got[b]
        self.over(b).start()

    def third(self, b, extra):
        self.over(b).wait()
        self.total[self.mine(b)] = self.half[b] + self.far[b] + extra(self.mine(b))
        self.back(b).start()

    def last(self, b):
        self.back(b).wait()


MEM_SCRATCH = [pltpu.VMEM((BLOCKS, 4, 32, 128), F32)] * 3 + [pltpu.SemaphoreType.DMA((3, BLOCKS))] * 2


def route_ranks(cnt_ref, owner_ref, col_ref, lev_ref, frac_ref, inn_ref, rinv_ref, tgt_ref, high_ref, low_ref, term_ref):
    rows, wide = owner_ref.shape
    place = iota((rows, wide), 0) * wide + iota((rows, wide), 1)
    live = place < cnt_ref[0]
    owner = jnp.where(live, owner_ref[...], GROUPS)
    level = lev_ref[...]
    key = (owner * 32 + level).astype(F32)
    turned = jnp.concatenate([key, key], 0).T
    earlier = iota((wide, wide), 0) < iota((wide, wide), 1)
    one_if = lambda cond: jnp.where(cond, 1.0, 0.0).astype(BF16)
    owners = [one_if(iota((GROUPS, wide), 0) == owner[c:c + 1]) for c in range(rows)]
    levels = [one_if(iota((32, wide), 0) == level[c:c + 1]) for c in range(rows)]
    running = jnp.zeros((GROUPS, 32), F32)
    starts = []
    for c in range(rows):
        starts.append(running)
        running = running + mm(owners[c], levels[c], NT)
    lower = one_if(iota((32, 32), 0) < iota((32, 32), 1))
    hi, lo = split(running)
    offset = mm(hi, lower) + mm(lo, lower)
    ranks = []
    for c in range(rows):
        hi, lo = split(offset + starts[c])
        both = mm(jnp.concatenate([hi, lo], 0), levels[c])
        same = jnp.where((turned[:, c:c + 1] == key[c:c + 1]) & earlier, 1.0, 0.0)
        at = (both[:GROUPS] + both[GROUPS:]) * owners[c].astype(F32)
        ranks.append(jnp.sum(at, 0, keepdims=True) + jnp.sum(same, 0, keepdims=True))
    rank = jnp.where(live, jnp.concatenate(ranks, 0).astype(jnp.int32), 0)
    tgt_ref[...] = jnp.where(live, owner * 512 + rank, -1)
    high_ref[...] = jnp.where(live, rank // 128 * GROUPS + owner, -1)
    low_ref[...] = rank % 128
    base = (lev_ref[...] * 4096 + col_ref[...]).astype(F32)
    for at, v in ((3, inn_ref[...]), (4, rinv_ref[...]), (5, base)):
        hi, lo = split(v)
        term_ref[2 * at] = hi.astype(F32)
        term_ref[2 * at + 1] = lo.astype(F32)
    for at in range(3):
        for r in range(rows):
            hi, lo = split(frac_ref[at:at + 1, wide * r:wide * (r + 1)])
            term_ref[2 * at, r:r + 1] = hi.astype(F32)
            term_ref[2 * at + 1, r:r + 1] = lo.astype(F32)


def route_slots(high_ref, low_ref, term_ref, acc_ref, out_ref):
    acc_ref[...] = jnp.zeros_like(acc_ref)

    def one(c, carry):
        def pair(ref, *at):
            r = 2 * c
            return jnp.concatenate([ref[(*at, pl.ds(r, 1), slice(None))], ref[(*at, pl.ds(r + 1, 1), slice(None))]], 1)

        hit = jnp.where(iota((128, 256), 0) == pair(high_ref), 1.0, 0.0).astype(BF16)
        lane = jnp.where(iota((128, 256), 0) == pair(low_ref), 1.0, 0.0).astype(BF16)
        stack = jnp.concatenate([lane * pair(term_ref, t).astype(BF16) for t in range(12)], 0)
        acc_ref[...] += mm(hit, stack, NT)
        return carry

    lax.fori_loop(0, 32, one, 0, unroll=2)
    for ch in range(6):
        full = acc_ref[:, 256 * ch:256 * ch + 128] + acc_ref[:, 256 * ch + 128:256 * ch + 256]
        for q in range(4):
            out_ref[:, ch * 4 + q, :] = full[q * GROUPS:(q + 1) * GROUPS]


def unroute(tgt_ref, ret, out_ref):
    rows = tgt_ref.shape[0]
    hi, lo = split(ret.T)
    table = jnp.concatenate([hi, lo], 0)
    for c in range(0, rows, 2):
        tgt = jnp.concatenate([tgt_ref[c:c + 1], tgt_ref[c + 1:c + 2]], 1)
        hit = jnp.where(iota((128, 256), 0) == tgt // 128, 1.0, 0.0).astype(BF16)
        picked = mm(table, hit)
        picked = picked[:128] + picked[128:]
        row = jnp.sum(jnp.where((iota((128, 256), 0) == tgt % 128) & (tgt >= 0), picked, 0.0), 0, keepdims=True)
        out_ref[c:c + 1] = row[:, :128]
        out_ref[c + 1:c + 2] = row[:, 128:]


def diffuse_rows(field):
    near = field[:-2] + field[2:]
    mid = field[1:-1]
    near = near + pltpu.roll(mid, 1, 1) + pltpu.roll(mid, 47, 1)
    return mid + NU * (near - 4.0 * mid)


def mixing(lv):
    tiled = jnp.concatenate([jnp.concatenate([lv] * 4, 1)] * 4, 0)
    return jnp.where(iota((128, 128), 0) // 32 == iota((128, 128), 1) // 32, tiled, 0.0)


def three(a, b):
    hi, lo = split(a)
    bhi, blo = split(b)
    return mm(jnp.concatenate([hi, lo, hi], 1), jnp.concatenate([bhi, bhi, blo], 0))


def forward_kernel(
    cnt_ref, owner_ref, col_ref, lev_ref, frac_ref, inn_ref, rinv_ref, alpha_ref, pert_hbm, bg_ref, static_ref, lv_ref, sy_ref, sx_ref,
    table_ref, obs_ref, order_ref, tgt_ref,
    inc_ref, ext_ref, pert_ref, turn_ref, part_ref, out_ref, high_ref, low_ref, term_ref, acc_ref,
    half_ref, got_ref, far_ref, msend, mrecv,
    xsend, xrecv, ysend, yrecv, osend, orecv, own,
):
    place = Place()

    def x_copies(g):
        lanes = pl.ds(pl.multiple_of(g * 128, 128), 128)
        return (
            remote(alpha_ref.at[4:8, :, lanes], ext_ref.at[g, 0:4, 8:40], xsend.at[0, g], xrecv.at[0, g], place.below),
            remote(alpha_ref.at[0:5, :, lanes], ext_ref.at[g, 12:17, 8:40], xsend.at[1, g], xrecv.at[1, g], place.above),
        )

    def y_copies(g):
        return (
            remote(ext_ref.at[g, :, 32:40], ext_ref.at[g, :, 0:8], ysend.at[0, g], yrecv.at[0, g], place.right),
            remote(ext_ref.at[g, :, 8:16], ext_ref.at[g, :, 40:48], ysend.at[1, g], yrecv.at[1, g], place.left),
        )

    def own_copy(g):
        lanes = pl.ds(pl.multiple_of(g * 128, 128), 128)
        return pltpu.make_async_copy(alpha_ref.at[:, :, lanes], ext_ref.at[g, 4:12, 8:40], own.at[g])

    pert_copy = pltpu.make_async_copy(pert_hbm, pert_ref, own.at[CHUNKS])
    exchange = Exchange(place, out_ref, obs_ref, osend, orecv, own.at[CHUNKS + 1])
    total = MemSum(place, part_ref, inc_ref, half_ref, got_ref, far_ref, msend, mrecv)

    place.greet()

    def begin(g, carry):
        for copy in x_copies(g):
            copy.start()
        own_copy(g).start()
        return carry

    lax.fori_loop(0, CHUNKS, begin, 0)
    pert_copy.start()
    turn_ref[...] = jnp.zeros_like(turn_ref)
    route_ranks(cnt_ref, owner_ref, col_ref, lev_ref, frac_ref, inn_ref, rinv_ref, tgt_ref, high_ref, low_ref, term_ref)
    route_slots(high_ref, low_ref, term_ref, acc_ref, out_ref)

    exchange.start()
    mix = mixing(lv_ref[...]).T

    def sideways(g):
        for copy in x_copies(g):
            copy.wait()
        own_copy(g).wait()
        for copy in y_copies(g):
            copy.start()

    def smooth(g):
        for copy in y_copies(g):
            copy.wait()
        field = ext_ref[g]
        for step in range(4):
            field = diffuse_rows(field)
        field = three(field[:, 8:48].reshape(9 * 40, 128), mix).reshape(9, 40, 128)
        for a in range(9):
            hi, lo = split(field[a])
            turn_ref[pl.ds(pl.multiple_of(g * 128, 128), 128), a, :] = mm(jnp.concatenate([hi, lo], 0), sy_ref[...], TN)

    def both(g, carry):
        sideways(g)
        smooth(g - 1)
        return carry

    sideways(0)
    lax.fori_loop(1, CHUNKS, both, 0)
    smooth(CHUNKS - 1)
    pert_copy.wait()

    def block(b):
        def member(k, carry):
            hi, lo = split(turn_ref[pl.ds(k * 32 + 8 * b, 8)].reshape(128, 128))
            fine = mm(sx_ref[...], jnp.concatenate([hi, lo], 0)).reshape(8, 32, 128)
            return carry + fine * pert_ref[k, 8 * b:8 * b + 8].astype(F32)

        part_ref[8 * b:8 * b + 8] = lax.fori_loop(0, 20, member, jnp.zeros((8, 32, 128), F32), unroll=4)

    extra = lambda at: bg_ref[at] * static_ref[at]
    for s in range(BLOCKS + 3):
        if s < BLOCKS:
            block(s)
            total.near(s).start()
        if 0 <= s - 1 < BLOCKS:
            total.second(s - 1)
        if s == BLOCKS:
            exchange.wait()
            order_ref[...] = chunk_order(obs_ref)
        if 0 <= s - 2 < BLOCKS:
            total.third(s - 2, extra)
        if 0 <= s - 3 < BLOCKS:
            b = s - 3
            total.last(b)
            hi, lo = split(inc_ref[8 * b:8 * b + 8].reshape(256, 128).T)
            table_ref[b, 0:128] = hi
            table_ref[b, 128:256] = lo


VMEM = pl.BlockSpec(memory_space=pltpu.VMEM)
SMEM = pl.BlockSpec(memory_space=pltpu.SMEM)
ANY = pl.BlockSpec(memory_space=pl.ANY)
DMA = pltpu.SemaphoreType.DMA


def forward(cnt, owner, col, lev, frac, inn, rinv, alpha, pert, bg, static, lv, sy, sx):
    return pl.pallas_call(
        forward_kernel,
        out_shape=(
            jax.ShapeDtypeStruct((BLOCKS, 256, 256), BF16),
            jax.ShapeDtypeStruct((GROUPS, 24, 128), F32),
            jax.ShapeDtypeStruct((8, 128), jnp.int32),
            jax.ShapeDtypeStruct((64, 128), jnp.int32),
        ),
        in_specs=[SMEM] + [VMEM] * 6 + [ANY] * 2 + [VMEM] * 5,
        out_specs=(VMEM,) * 4,
        scratch_shapes=[
            pltpu.VMEM((32, 32, 128), F32),
            pltpu.VMEM((CHUNKS, 17, 48, 128), F32),
            pltpu.VMEM(pert.shape, BF16),
            pltpu.VMEM((640, 16, 128), F32),
            pltpu.VMEM((32, 32, 128), F32),
            pltpu.VMEM((GROUPS, 24, 128), F32),
            pltpu.VMEM((64, 128), jnp.int32),
            pltpu.VMEM((64, 128), jnp.int32),
            pltpu.VMEM((12, 64, 128), F32),
            pltpu.VMEM((128, 1536), F32),
        ] + MEM_SCRATCH + [DMA((2, CHUNKS))] * 4 + [DMA((GROUPS,))] * 2 + [DMA((CHUNKS + 2,))],
        compiler_params=pltpu.CompilerParams(vmem_limit_bytes=VMEM_LIMIT, collective_id=0, has_side_effects=True),
        name="forward",
    )(cnt, owner, col, lev, frac, inn, rinv, alpha, pert, bg, static, lv, sy, sx)


def backward_kernel(
    adj_ref, dep_ref, tgt_ref, pert_hbm, lv_ref, gy_ref, gx_ref,
    grad_ref, full_ref, depout_ref,
    pert_ref, turn_ref, wide_ref, fromleft_ref, fromright_ref, fromabove_ref, frombelow_ref, ret_ref,
    half_ref, got_ref, far_ref, msend, mrecv,
    xsend, xrecv, ysend, yrecv, osend, orecv, own,
):
    place = Place()

    def y_copies(g):
        return (
            remote(wide_ref.at[g, :, 40:48], fromleft_ref.at[g], ysend.at[0, g], yrecv.at[0, g], place.right),
            remote(wide_ref.at[g, :, 0:8], fromright_ref.at[g], ysend.at[1, g], yrecv.at[1, g], place.left),
        )

    def x_copies(g):
        return (
            remote(wide_ref.at[g, 12:17, 8:40], fromabove_ref.at[g], xsend.at[0, g], xrecv.at[0, g], place.below),
            remote(wide_ref.at[g, 0:4, 8:40], frombelow_ref.at[g], xsend.at[1, g], xrecv.at[1, g], place.above),
        )

    pert_copy = pltpu.make_async_copy(pert_hbm, pert_ref, own.at[0])
    exchange = Exchange(place, dep_ref, ret_ref, osend, orecv, own.at[1])
    total = MemSum(place, adj_ref, full_ref, half_ref, got_ref, far_ref, msend, mrecv)

    place.greet()
    for b in range(BLOCKS):
        total.near(b).start()
    pert_copy.start()
    for b in range(BLOCKS):
        total.second(b)
    exchange.start()
    pert_copy.wait()

    def block(b):
        fine_adj = full_ref[8 * b:8 * b + 8]

        def member(k, carry):
            fine = fine_adj * pert_ref[k, 8 * b:8 * b + 8].astype(F32)
            hi, lo = split(fine.reshape(256, 128))
            turn_ref[pl.ds(k * 32 + 8 * b, 8)] = mm(gx_ref[...], jnp.concatenate([hi, lo], 0)).reshape(8, 16, 128)
            return carry

        lax.fori_loop(0, 20, member, 0, unroll=4)

    for s in range(BLOCKS + 1):
        if s < BLOCKS:
            total.third(s, lambda at: 0.0)
        if s >= 1:
            total.last(s - 1)
            block(s - 1)

    mix = mixing(lv_ref[...])

    def smooth(g, carry):
        rows = []
        for a in range(9):
            hi, lo = split(turn_ref[pl.ds(pl.multiple_of(g * 128, 128), 128), a, :])
            rows.append(mm(gy_ref[...], jnp.concatenate([hi, lo], 1), NT))
        field = three(jnp.concatenate(rows, 0), mix).reshape(9, 40, 128)
        field = jnp.concatenate([jnp.zeros((9, 8, 128), F32), field], 1)
        for step in range(4):
            two = jnp.zeros((2, 48, 128), F32)
            field = diffuse_rows(jnp.concatenate([two, field, two], 0))
        wide_ref[g] = field
        for copy in y_copies(g):
            copy.start()
        return carry

    def lengthways(g, carry):
        for copy in y_copies(g):
            copy.wait()
        wide_ref[g, :, 8:16] += fromleft_ref[g]
        wide_ref[g, :, 32:40] += fromright_ref[g]
        for copy in x_copies(g):
            copy.start()
        return carry

    def both(g, carry):
        smooth(g, carry)
        return lengthways(g - 1, carry)

    smooth(0, 0)
    lax.fori_loop(1, CHUNKS, both, 0)
    lengthways(CHUNKS - 1, 0)

    exchange.wait()
    unroute(tgt_ref, ret_ref[...].reshape(128, 128), depout_ref)
    for g in range(CHUNKS):
        for copy in x_copies(g):
            copy.wait()
        lanes = slice(128 * g, 128 * g + 128)
        grad_ref[:, :, lanes] = wide_ref[g, 4:12, 8:40]
        grad_ref[0:5, :, lanes] += fromabove_ref[g]
        grad_ref[4:8, :, lanes] += frombelow_ref[g]


def backward(adj, dep, tgt, pert, lv, gy, gx):
    return pl.pallas_call(
        backward_kernel,
        out_shape=(
            jax.ShapeDtypeStruct((8, 32, 640), F32),
            jax.ShapeDtypeStruct((32, 32, 128), F32),
            jax.ShapeDtypeStruct(tgt.shape, F32),
        ),
        in_specs=[VMEM] * 3 + [ANY] + [VMEM] * 3,
        out_specs=(VMEM,) * 3,
        scratch_shapes=[
            pltpu.VMEM(pert.shape, BF16),
            pltpu.VMEM((640, 16, 128), F32),
            pltpu.VMEM((CHUNKS, 17, 48, 128), F32),
            pltpu.VMEM((CHUNKS, 17, 8, 128), F32),
            pltpu.VMEM((CHUNKS, 17, 8, 128), F32),
            pltpu.VMEM((CHUNKS, 5, 32, 128), F32),
            pltpu.VMEM((CHUNKS, 4, 32, 128), F32),
            pltpu.VMEM((GROUPS, 4, 128), F32),
        ] + MEM_SCRATCH + [DMA((2, CHUNKS))] * 4 + [DMA((GROUPS,))] * 2 + [DMA((2,))],
        compiler_params=pltpu.CompilerParams(vmem_limit_bytes=VMEM_LIMIT, collective_id=1, has_side_effects=True),
        name="backward",
    )(adj, dep, tgt, pert, lv, gy, gx)


def finish_kernel(alpha_ref, back_ref, bg_ref, static_ref, adj_ref, dep_ref, grad_ref, gstat_ref, out_ref):
    grad_ref[...] = alpha_ref[...] + back_ref[...]
    gstat_ref[...] = static_ref[...] + bg_ref[...] * adj_ref[...]
    out_ref[...] = dep_ref[...]


def finish(alpha, back, bg, static, adj, dep):
    return pl.pallas_call(
        finish_kernel,
        out_shape=tuple(jax.ShapeDtypeStruct(a.shape, F32) for a in (alpha, static, dep)),
        in_specs=[VMEM] * 6,
        out_specs=(VMEM,) * 3,
        compiler_params=pltpu.CompilerParams(vmem_limit_bytes=VMEM_LIMIT),
        name="finish",
    )(alpha, back, bg, static, adj, dep)


def per_device(alpha, lv_sqrt, ens_pert, bg_sigma, static_ctrl, obs_owner, obs_column, obs_level, obs_frac, innovation, obs_rinv, obs_count):
    spread_y, gather_y, spread_x, gather_x = tables()
    shape = (64, 128)
    table, incoming, order, target = forward(
        obs_count, obs_owner.reshape(shape), obs_column.reshape(shape), obs_level.reshape(shape), obs_frac,
        innovation.reshape(shape), obs_rinv.reshape(shape), alpha, ens_pert, bg_sigma, static_ctrl, lv_sqrt, spread_y, spread_x,
    )
    departure, adjoint = stencil(order, table, incoming)
    back, adjoint, departures = backward(adjoint.reshape(32, 32, 128), departure, target, ens_pert, lv_sqrt, gather_y, gather_x)
    grad_alpha, grad_static, departures = finish(alpha, back, bg_sigma, static_ctrl, adjoint, departures)
    return grad_alpha, grad_static, departures.reshape(-1)


def solution(mesh):
    placed = (
        P("tx", "ty", "mem"),
        P(),
        P("mem", None, "tx", "ty"),
        P(None, "tx", "ty"),
        P(None, "tx", "ty"),
        P(("tx", "ty", "mem"), None),
        P(("tx", "ty", "mem")),
        P(("tx", "ty", "mem")),
        P(None, ("tx", "ty", "mem")),
        P(("tx", "ty", "mem")),
        P(("tx", "ty", "mem")),
        P(("tx", "ty", "mem")),
    )
    return jax.shard_map(
        per_device,
        mesh=mesh,
        in_specs=placed,
        out_specs=(P("tx", "ty", "mem"), P(None, "tx", "ty"), P(("tx", "ty", "mem"))),
        check_vma=False,
    )
```

```python
import functools
import numpy as np
import jax
import jax.numpy as jnp
from jax import lax
from jax.experimental import pallas as pl
from jax.experimental.pallas import tpu as pltpu
from jax.sharding import PartitionSpec as P

F32 = jnp.float32
BF16 = jnp.bfloat16
NU = 0.2
RATIO = 4
VMEM_LIMIT = 56 * 1024 * 1024
NN = (((1,), (0,)), ((), ()))
NT = (((1,), (1,)), ((), ()))
TN = (((0,), (0,)), ((), ()))


def mm(a, b, dims=NN):
    return lax.dot_general(a, b, dims, preferred_element_type=F32)


def split(v):
    hi = v.astype(BF16)
    return hi, (v - hi.astype(F32)).astype(BF16)


def iota(shape, dim):
    return lax.broadcasted_iota(jnp.int32, shape, dim)


def tent(position, count):
    return jnp.maximum(1.0 - jnp.abs(position - iota((count, 128), 0).astype(F32)), 0.0)


def chunk_order(obs_ref):
    base = obs_ref[:, 20:24, :].astype(jnp.int32)
    live = obs_ref[:, 16:20, :] > 0.0
    level = base // 4096
    first = jnp.min(jnp.where(live, level, 99), 2, keepdims=True).astype(F32)
    last = jnp.max(jnp.where(live, level + 1, -1), 2, keepdims=True).astype(F32)
    spread = lambda v: jnp.broadcast_to(v, (32, 4, 128)).reshape(128, 128)
    first, last = spread(first), spread(last)
    down, along = iota((128, 128), 0), iota((128, 128), 1)
    key = first * 16384.0 + last * 128.0 + down.astype(F32)
    other = key.T
    rank = jnp.sum(jnp.where(other > key, 1.0, 0.0), 0, keepdims=True)
    hit = along == jnp.broadcast_to(rank, (128, 128)).T.astype(jnp.int32)
    pick = lambda v: jnp.sum(jnp.where(hit, v, 0.0), 0, keepdims=True)
    live_count = jnp.sum(jnp.where(other < 98.0 * 16384.0, 1.0, 0.0), 1, keepdims=True)
    count = jnp.broadcast_to(live_count, (128, 128))[0:1]
    rows = [pick(down.astype(F32)), pick(first), pick(last), count]
    return jnp.concatenate(rows + [jnp.zeros((4, 128), F32)], 0).astype(jnp.int32)


def stencil_kernel(order_ref, table_ref, obs_ref, dep_ref, adj_ref, acc_ref, ahi0, alo0, ahi1, alo1, place_ref, in_x_ref, in_y_ref, sum_ref, spread_ref, where_ref):
    slots = ((ahi0, alo0), (ahi1, alo1))
    acc_ref[...] = jnp.zeros_like(acc_ref)
    dep_ref[...] = jnp.zeros_like(dep_ref)
    ahi1[0:512] = jnp.zeros((512, 512), BF16)
    alo1[0:512] = jnp.zeros((512, 512), BF16)
    base = obs_ref[:, 20:24, :].astype(jnp.int32)
    where_ref[:, 0:4] = (base >> 12).astype(F32) + obs_ref[:, 8:12, :]
    where_ref[:, 4:8] = ((base >> 7) & 31).astype(F32) + obs_ref[:, 0:4, :]
    where_ref[:, 8:12] = (base & 127).astype(F32) + obs_ref[:, 4:8, :]
    spread_ref[...] = jnp.zeros_like(spread_ref)
    groups = (order_ref[3, 0] + 3) // 4

    def lanes(start, step, wide):
        return pl.ds(pl.multiple_of((start + step) * 128, 128), wide)

    def adjoint(slot, at, rows):
        acc_ref[0:256, at] += mm(spread_ref[...], slots[slot][0][rows], NT)
        acc_ref[256:384, at] += mm(spread_ref[0:128], slots[slot][1][rows], NT)

    def more(start, rest, what):
        def one(g, carry):
            what(lanes(start, 4 + 2 * g, 256), pl.ds(pl.multiple_of(512 + 256 * g, 256), 256), 16 + 8 * g)
            return carry

        lax.fori_loop(0, rest, one, 0)

    def one_group(n, slot, before):
        ahi_ref, alo_ref = slots[slot]
        old_start, old_rest = before
        first_of = jnp.minimum(4 * n, 124)
        first = order_ref[1, first_of]
        last = order_ref[2, first_of]
        for j in range(1, 4):
            first = jnp.minimum(first, order_ref[1, first_of + j])
            last = jnp.maximum(last, order_ref[2, first_of + j])
        start = jnp.minimum(first // 4, 4)
        rest = jnp.maximum(last - 4 * start - 16 + 8, 0) // 8
        rest = jnp.where(n < groups, rest, 0)

        adjoint(1 - slot, lanes(old_start, 0, 512), slice(0, 512))
        sources, parts = [], []
        for j in range(4):
            chunk = order_ref[0, first_of + j]
            s, q = chunk // 4, lax.rem(chunk, 4)
            sources.append(s)
            parts.append(q)
            get = lambda ch: where_ref[s, pl.ds(ch * 4 + q, 1), :]
            at = slice(128 * j, 128 * j + 128)
            place_ref[:, at] = jnp.broadcast_to(get(0) - (4 * start).astype(F32), (8, 128))
            in_x_ref[:, at] = tent(get(1), 32)
            in_y_ref[:, at] = tent(get(2), 128)

        def build(row, level):
            far = place_ref[...] - (iota((8, 512), 0) + level).astype(F32)
            in_l = jnp.maximum(1.0 - jnp.abs(far), 0.0)
            for l in range(8):
                hi, lo = split(in_l[l:l + 1] * in_x_ref[...])
                at = pl.ds(row + 32 * l, 32)
                ahi_ref[at] = hi
                alo_ref[at] = lo

        build(0, 0)
        build(256, 8)
        table = table_ref[:, lanes(start, 0, 512)]
        both = mm(table, ahi_ref[0:512])
        sum_ref[...] = both[:128] + both[128:] + mm(table[:128], alo_ref[0:512])

        def gather(at, rows, level):
            build(pl.multiple_of(32 * level, 256), level)
            table = table_ref[:, at]
            both = mm(table, ahi_ref[rows])
            sum_ref[...] += both[:128] + both[128:] + mm(table[:128], alo_ref[rows])

        more(old_start, old_rest, lambda at, rows, level: adjoint(1 - slot, at, rows))
        more(start, rest, gather)

        for j in range(4):
            at = slice(128 * j, 128 * j + 128)
            get = lambda ch: obs_ref[sources[j], pl.ds(ch * 4 + parts[j], 1), :]
            dep = jnp.sum(sum_ref[:, at] * in_y_ref[:, at], 0, keepdims=True) - get(3)
            dep_ref[sources[j], pl.ds(parts[j], 1), :] = dep
            hi, lo = split(in_y_ref[:, at] * (dep * get(4)))
            spread_ref[0:128, at] = hi
            spread_ref[128:256, at] = lo
        return start, rest

    def two_groups(i, before):
        return one_group(2 * i + 1, 1, one_group(2 * i, 0, before))

    start, rest = lax.fori_loop(0, (groups + 1) // 2, two_groups, (jnp.int32(0), jnp.int32(0)))
    adjoint(1, lanes(start, 0, 512), slice(0, 512))
    more(start, rest, lambda at, rows, level: adjoint(1, at, rows))
    adj_ref[...] = (acc_ref[0:128, 0:1024] + acc_ref[128:256, 0:1024] + acc_ref[256:384, 0:1024]).T


def stencil(order, table, obs):
    return pl.pallas_call(
        stencil_kernel,
        out_shape=(jax.ShapeDtypeStruct((32, 4, 128), F32), jax.ShapeDtypeStruct((1024, 128), F32)),
        in_specs=[pl.BlockSpec(memory_space=pltpu.SMEM)] + [pl.BlockSpec(memory_space=pltpu.VMEM)] * 2,
        out_specs=(pl.BlockSpec(memory_space=pltpu.VMEM),) * 2,
        scratch_shapes=[
            pltpu.VMEM((384, 1280), F32),
            pltpu.VMEM((1280, 512), BF16),
            pltpu.VMEM((1280, 512), BF16),
            pltpu.VMEM((1280, 512), BF16),
            pltpu.VMEM((1280, 512), BF16),
            pltpu.VMEM((8, 512), F32),
            pltpu.VMEM((32, 512), F32),
            pltpu.VMEM((128, 512), F32),
            pltpu.VMEM((128, 512), F32),
            pltpu.VMEM((256, 512), BF16),
            pltpu.VMEM((32, 16, 128), F32),
        ],
        compiler_params=pltpu.CompilerParams(vmem_limit_bytes=VMEM_LIMIT),
        name="stencil",
    )(order, table, obs)


def line_weights(fine, coarse):
    out = np.zeros((fine, coarse), np.float32)
    for f in range(fine):
        out[f, f // RATIO] += 1.0 - (f % RATIO) / RATIO
        out[f, f // RATIO + 1] += (f % RATIO) / RATIO
    return out


def tables():
    along = line_weights(128, 40)
    across = line_weights(32, 16)
    spread_y = np.concatenate([along.T, along.T], 0)
    gather_y = np.concatenate([along.T, along.T], 1)
    eye = np.eye(8, dtype=np.float32)
    block = np.kron(eye, across)
    spread_x = np.concatenate([block, block], 1)
    gather_x = np.concatenate([block.T, block.T], 1)
    return [jnp.asarray(t, BF16) for t in (spread_y, gather_y, spread_x, gather_x)]


def diffuse_rows(field, first, last):
    near = field[first - 1:last - 1] + field[first + 1:last + 1]
    mid = field[first:last]
    near = near + pltpu.roll(mid, 1, 1) + pltpu.roll(mid, 47, 1)
    return mid + NU * (near - 4.0 * mid)


def three(a, b_ref):
    hi, lo = split(a)
    return mm(jnp.concatenate([hi, lo, hi], 1), b_ref[...])

MESH = pl.DeviceIdType.MESH
GROUPS = 32
CHUNKS = 5
BLOCKS = 4


def tile_id(index, mem):
    return (index // 4, index % 4, mem)


def remote(src, dst, send, recv, device):
    return pltpu.make_async_remote_copy(src_ref=src, dst_ref=dst, send_sem=send, recv_sem=recv, device_id=device, device_id_type=MESH)


class Place:
    def __init__(self):
        self.tx, self.ty, self.mem = lax.axis_index("tx"), lax.axis_index("ty"), lax.axis_index("mem")
        self.tile = self.tx * 4 + self.ty
        self.core = self.mem % 2
        self.below = (lax.rem(self.tx + 1, 8), self.ty, self.mem)
        self.above = (lax.rem(self.tx + 7, 8), self.ty, self.mem)
        self.right = (self.tx, lax.rem(self.ty + 1, 4), self.mem)
        self.left = (self.tx, lax.rem(self.ty + 3, 4), self.mem)
        self.twin = (self.tx, self.ty, self.mem + 1 - 2 * self.core)
        self.across = (self.tx, self.ty, lax.rem(self.mem + 2, 4))

    def greet(self):
        barrier = pltpu.get_barrier_semaphore()

        def one(d, carry):
            other = lax.rem(self.tile + d, GROUPS)
            pl.semaphore_signal(barrier, inc=1, device_id=tile_id(other, self.mem), device_id_type=MESH)
            return carry

        lax.fori_loop(1, GROUPS, one, 0)
        for other in (self.twin, self.across):
            pl.semaphore_signal(barrier, inc=1, device_id=other, device_id_type=MESH)
        pl.semaphore_wait(barrier, GROUPS + 1)


class Exchange:
    def __init__(self, place, src, dst, send, recv, own):
        self.place, self.src, self.dst, self.send, self.recv = place, src, dst, send, recv
        self.own = pltpu.make_async_copy(src.at[place.tile], dst.at[place.tile], own)

    def copy(self, d):
        other = lax.rem(self.place.tile + d, GROUPS)
        return remote(self.src.at[other], self.dst.at[self.place.tile], self.send.at[d], self.recv.at[d], tile_id(other, self.place.mem))

    def start(self):
        self.own.start()

        def one(d, carry):
            self.copy(d).start()
            return carry

        lax.fori_loop(1, GROUPS, one, 0)

    def wait(self):
        self.own.wait()

        def one(d, carry):
            self.copy(d).wait()
            return carry

        lax.fori_loop(1, GROUPS, one, 0)


class MemSum:
    def __init__(self, place, part, total, half, got, far, send, recv):
        self.place, self.part, self.total = place, part, total
        self.half, self.got, self.far, self.send, self.recv = half, got, far, send, recv

    def mine(self, b):
        return pl.ds(8 * b + 4 * self.place.core, 4)

    def near(self, b):
        return remote(self.part.at[pl.ds(8 * b + 4 - 4 * self.place.core, 4)], self.got.at[b], self.send.at[0, b], self.recv.at[0, b], self.place.twin)

    def over(self, b):
        return remote(self.half.at[b], self.far.at[b], self.send.at[1, b], self.recv.at[1, b], self.place.across)

    def back(self, b):
        return remote(self.total.at[self.mine(b)], self.total.at[self.mine(b)], self.send.at[2, b], self.recv.at[2, b], self.place.twin)

    def second(self, b):
        self.near(b).wait()
        self.half[b] = self.part[self.mine(b)] + self.got[b]
        self.over(b).start()

    def third(self, b, extra):
        self.over(b).wait()
        self.total[self.mine(b)] = self.half[b] + self.far[b] + extra(self.mine(b))
        self.back(b).start()

    def last(self, b):
        self.back(b).wait()


MEM_SCRATCH = [pltpu.VMEM((BLOCKS, 4, 32, 128), F32)] * 3 + [pltpu.SemaphoreType.DMA((3, BLOCKS))] * 2


def route_ranks(cnt_ref, owner_ref, col_ref, lev_ref, frac_ref, inn_ref, rinv_ref, tgt_ref, high_ref, low_ref, term_ref):
    rows, wide = owner_ref.shape
    place = iota((rows, wide), 0) * wide + iota((rows, wide), 1)
    live = place < cnt_ref[0]
    owner = jnp.where(live, owner_ref[...], GROUPS)
    level = lev_ref[...]
    key = (owner * 32 + level).astype(F32)
    turned = jnp.concatenate([key, key], 0).T
    earlier = iota((wide, wide), 0) < iota((wide, wide), 1)
    one_if = lambda cond: jnp.where(cond, 1.0, 0.0).astype(BF16)
    owners = [one_if(iota((GROUPS, wide), 0) == owner[c:c + 1]) for c in range(rows)]
    levels = [one_if(iota((32, wide), 0) == level[c:c + 1]) for c in range(rows)]
    running = jnp.zeros((GROUPS, 32), F32)
    starts = []
    for c in range(rows):
        starts.append(running)
        running = running + mm(owners[c], levels[c], NT)
    lower = one_if(iota((32, 32), 0) < iota((32, 32), 1))
    hi, lo = split(running)
    offset = mm(hi, lower) + mm(lo, lower)
    ranks = []
    for c in range(rows):
        hi, lo = split(offset + starts[c])
        both = mm(jnp.concatenate([hi, lo], 0), levels[c])
        same = jnp.where((turned[:, c:c + 1] == key[c:c + 1]) & earlier, 1.0, 0.0)
        at = (both[:GROUPS] + both[GROUPS:]) * owners[c].astype(F32)
        ranks.append(jnp.sum(at, 0, keepdims=True) + jnp.sum(same, 0, keepdims=True))
    rank = jnp.where(live, jnp.concatenate(ranks, 0).astype(jnp.int32), 0)
    tgt_ref[...] = jnp.where(live, owner * 512 + rank, -1)
    high_ref[...] = jnp.where(live, rank // 128 * GROUPS + owner, -1)
    low_ref[...] = rank % 128
    base = (lev_ref[...] * 4096 + col_ref[...]).astype(F32)
    for at, v in ((3, inn_ref[...]), (4, rinv_ref[...]), (5, base)):
        hi, lo = split(v)
        term_ref[2 * at] = hi.astype(F32)
        term_ref[2 * at + 1] = lo.astype(F32)
    for at in range(3):
        for r in range(rows):
            hi, lo = split(frac_ref[at:at + 1, wide * r:wide * (r + 1)])
            term_ref[2 * at, r:r + 1] = hi.astype(F32)
            term_ref[2 * at + 1, r:r + 1] = lo.astype(F32)


def route_slots(high_ref, low_ref, term_ref, acc_ref, out_ref):
    acc_ref[...] = jnp.zeros_like(acc_ref)

    def one(c, carry):
        def pair(ref, *at):
            r = 2 * c
            return jnp.concatenate([ref[(*at, pl.ds(r, 1), slice(None))], ref[(*at, pl.ds(r + 1, 1), slice(None))]], 1)

        hit = jnp.where(iota((128, 256), 0) == pair(high_ref), 1.0, 0.0).astype(BF16)
        lane = jnp.where(iota((128, 256), 0) == pair(low_ref), 1.0, 0.0).astype(BF16)
        stack = jnp.concatenate([lane * pair(term_ref, t).astype(BF16) for t in range(12)], 0)
        acc_ref[...] += mm(hit, stack, NT)
        return carry

    lax.fori_loop(0, 32, one, 0, unroll=2)
    for ch in range(6):
        full = acc_ref[:, 256 * ch:256 * ch + 128] + acc_ref[:, 256 * ch + 128:256 * ch + 256]
        for q in range(4):
            out_ref[:, ch * 4 + q, :] = full[q * GROUPS:(q + 1) * GROUPS]


def unroute(tgt_ref, ret, out_ref):
    rows = tgt_ref.shape[0]
    hi, lo = split(ret.T)
    table = jnp.concatenate([hi, lo], 0)
    for c in range(0, rows, 2):
        tgt = jnp.concatenate([tgt_ref[c:c + 1], tgt_ref[c + 1:c + 2]], 1)
        hit = jnp.where(iota((128, 256), 0) == tgt // 128, 1.0, 0.0).astype(BF16)
        picked = mm(table, hit)
        picked = picked[:128] + picked[128:]
        row = jnp.sum(jnp.where((iota((128, 256), 0) == tgt % 128) & (tgt >= 0), picked, 0.0), 0, keepdims=True)
        out_ref[c:c + 1] = row[:, :128]
        out_ref[c + 1:c + 2] = row[:, 128:]


def diffuse_rows(field):
    near = field[:-2] + field[2:]
    mid = field[1:-1]
    near = near + pltpu.roll(mid, 1, 1) + pltpu.roll(mid, 47, 1)
    return mid + NU * (near - 4.0 * mid)


def mixing(lv):
    tiled = jnp.concatenate([jnp.concatenate([lv] * 4, 1)] * 4, 0)
    return jnp.where(iota((128, 128), 0) // 32 == iota((128, 128), 1) // 32, tiled, 0.0)


def three(a, b):
    hi, lo = split(a)
    bhi, blo = split(b)
    return mm(jnp.concatenate([hi, lo, hi], 1), jnp.concatenate([bhi, bhi, blo], 0))


def forward_kernel(
    cnt_ref, owner_ref, col_ref, lev_ref, frac_ref, inn_ref, rinv_ref, alpha_ref, pert_hbm, bg_ref, static_ref, lv_ref, sy_ref, sx_ref,
    table_ref, obs_ref, order_ref, tgt_ref,
    inc_ref, ext_ref, pert_ref, turn_ref, part_ref, out_ref, high_ref, low_ref, term_ref, acc_ref,
    half_ref, got_ref, far_ref, msend, mrecv,
    xsend, xrecv, ysend, yrecv, osend, orecv, own,
):
    place = Place()

    def x_copies(g):
        lanes = pl.ds(pl.multiple_of(g * 128, 128), 128)
        return (
            remote(alpha_ref.at[4:8, :, lanes], ext_ref.at[g, 0:4, 8:40], xsend.at[0, g], xrecv.at[0, g], place.below),
            remote(alpha_ref.at[0:5, :, lanes], ext_ref.at[g, 12:17, 8:40], xsend.at[1, g], xrecv.at[1, g], place.above),
        )

    def y_copies(g):
        lanes = pl.ds(pl.multiple_of(g * 128, 128), 128)
        return (
            remote(alpha_ref.at[:, 24:32, lanes], ext_ref.at[g, 4:12, 0:8], ysend.at[0, g], yrecv.at[0, g], place.right),
            remote(alpha_ref.at[:, 0:8, lanes], ext_ref.at[g, 4:12, 40:48], ysend.at[1, g], yrecv.at[1, g], place.left),
        )

    def corner_copies(g):
        return (
            remote(ext_ref.at[g, 0:4, 32:40], ext_ref.at[g, 0:4, 0:8], ysend.at[2, g], yrecv.at[2, g], place.right),
            remote(ext_ref.at[g, 0:4, 8:16], ext_ref.at[g, 0:4, 40:48], ysend.at[3, g], yrecv.at[3, g], place.left),
            remote(ext_ref.at[g, 12:17, 32:40], ext_ref.at[g, 12:17, 0:8], ysend.at[4, g], yrecv.at[4, g], place.right),
            remote(ext_ref.at[g, 12:17, 8:16], ext_ref.at[g, 12:17, 40:48], ysend.at[5, g], yrecv.at[5, g], place.left),
        )

    def own_copy(g):
        lanes = pl.ds(pl.multiple_of(g * 128, 128), 128)
        return pltpu.make_async_copy(alpha_ref.at[:, :, lanes], ext_ref.at[g, 4:12, 8:40], own.at[g])

    pert_copy = pltpu.make_async_copy(pert_hbm, pert_ref, own.at[CHUNKS])
    exchange = Exchange(place, out_ref, obs_ref, osend, orecv, own.at[CHUNKS + 1])
    total = MemSum(place, part_ref, inc_ref, half_ref, got_ref, far_ref, msend, mrecv)

    place.greet()

    def begin(g, carry):
        for copy in x_copies(g) + y_copies(g):
            copy.start()
        own_copy(g).start()
        return carry

    lax.fori_loop(0, CHUNKS, begin, 0)
    pert_copy.start()
    turn_ref[...] = jnp.zeros_like(turn_ref)
    route_ranks(cnt_ref, owner_ref, col_ref, lev_ref, frac_ref, inn_ref, rinv_ref, tgt_ref, high_ref, low_ref, term_ref)
    route_slots(high_ref, low_ref, term_ref, acc_ref, out_ref)

    mix = mixing(lv_ref[...]).T
    part_ref[...] = jnp.zeros_like(part_ref)
    pert_copy.wait()

    def sideways(g):
        for copy in x_copies(g):
            copy.wait()
        for copy in corner_copies(g):
            copy.start()

    def smooth(g):
        own_copy(g).wait()
        for copy in y_copies(g) + corner_copies(g):
            copy.wait()
        field = ext_ref[g]
        for step in range(4):
            field = diffuse_rows(field)
        field = three(field[:, 8:48].reshape(9 * 40, 128), mix).reshape(9, 40, 128)
        for a in range(9):
            hi, lo = split(field[a])
            turn_ref[:, a, :] = mm(jnp.concatenate([hi, lo], 0), sy_ref[...], TN)
        for i in range(16):
            hi, lo = split(turn_ref[8 * i:8 * i + 8].reshape(128, 128))
            fine = mm(sx_ref[...], jnp.concatenate([hi, lo], 0)).reshape(8, 32, 128)
            l0 = i % 4 * 8
            part_ref[l0:l0 + 8] += fine * pert_ref[4 * g + i // 4, l0:l0 + 8].astype(F32)

    def both(g, carry):
        sideways(g)

        @pl.when(g == CHUNKS - 1)
        def _():
            exchange.start()

        smooth(g - 1)
        return carry

    sideways(0)
    lax.fori_loop(1, CHUNKS, both, 0)
    smooth(CHUNKS - 1)

    extra = lambda at: bg_ref[at] * static_ref[at]
    for b in range(BLOCKS):
        total.near(b).start()
    for b in range(BLOCKS):
        total.second(b)
    exchange.wait()
    order_ref[...] = chunk_order(obs_ref)
    for b in range(BLOCKS):
        total.third(b, extra)
    for b in range(BLOCKS):
        total.last(b)
        hi, lo = split(inc_ref[8 * b:8 * b + 8].reshape(256, 128).T)
        table_ref[0:128, 256 * b:256 * b + 256] = hi
        table_ref[128:256, 256 * b:256 * b + 256] = lo
    table_ref[:, 1024:1280] = jnp.zeros((256, 256), BF16)


VMEM = pl.BlockSpec(memory_space=pltpu.VMEM)
SMEM = pl.BlockSpec(memory_space=pltpu.SMEM)
ANY = pl.BlockSpec(memory_space=pl.ANY)
DMA = pltpu.SemaphoreType.DMA


def forward(cnt, owner, col, lev, frac, inn, rinv, alpha, pert, bg, static, lv, sy, sx):
    return pl.pallas_call(
        forward_kernel,
        out_shape=(
            jax.ShapeDtypeStruct((256, 1280), BF16),
            jax.ShapeDtypeStruct((GROUPS, 24, 128), F32),
            jax.ShapeDtypeStruct((8, 128), jnp.int32),
            jax.ShapeDtypeStruct((64, 128), jnp.int32),
        ),
        in_specs=[SMEM] + [VMEM] * 6 + [ANY] * 2 + [VMEM] * 5,
        out_specs=(VMEM,) * 4,
        scratch_shapes=[
            pltpu.VMEM((32, 32, 128), F32),
            pltpu.VMEM((CHUNKS, 17, 48, 128), F32),
            pltpu.VMEM(pert.shape, BF16),
            pltpu.VMEM((128, 16, 128), F32),
            pltpu.VMEM((32, 32, 128), F32),
            pltpu.VMEM((GROUPS, 24, 128), F32),
            pltpu.VMEM((64, 128), jnp.int32),
            pltpu.VMEM((64, 128), jnp.int32),
            pltpu.VMEM((12, 64, 128), F32),
            pltpu.VMEM((128, 1536), F32),
        ] + MEM_SCRATCH + [DMA((2, CHUNKS))] * 2 + [DMA((6, CHUNKS))] * 2 + [DMA((GROUPS,))] * 2 + [DMA((CHUNKS + 2,))],
        compiler_params=pltpu.CompilerParams(vmem_limit_bytes=VMEM_LIMIT, collective_id=0, has_side_effects=True),
        name="forward",
    )(cnt, owner, col, lev, frac, inn, rinv, alpha, pert, bg, static, lv, sy, sx)


def backward_kernel(
    adj_ref, dep_ref, tgt_ref, pert_hbm, lv_ref, gy_ref, gx_ref,
    grad_ref, full_ref, depout_ref,
    pert_ref, turn_ref, wide_ref, fromleft_ref, fromright_ref, fromabove_ref, frombelow_ref, ret_ref,
    half_ref, got_ref, far_ref, msend, mrecv,
    xsend, xrecv, ysend, yrecv, osend, orecv, own,
):
    place = Place()

    def y_copies(g):
        return (
            remote(wide_ref.at[g, :, 40:48], fromleft_ref.at[g], ysend.at[0, g], yrecv.at[0, g], place.right),
            remote(wide_ref.at[g, :, 0:8], fromright_ref.at[g], ysend.at[1, g], yrecv.at[1, g], place.left),
        )

    def x_copies(g):
        return (
            remote(wide_ref.at[g, 12:17, 8:40], fromabove_ref.at[g], xsend.at[0, g], xrecv.at[0, g], place.below),
            remote(wide_ref.at[g, 0:4, 8:40], frombelow_ref.at[g], xsend.at[1, g], xrecv.at[1, g], place.above),
        )

    pert_copy = pltpu.make_async_copy(pert_hbm, pert_ref, own.at[0])
    exchange = Exchange(place, dep_ref, ret_ref, osend, orecv, own.at[1])
    total = MemSum(place, adj_ref, full_ref, half_ref, got_ref, far_ref, msend, mrecv)

    place.greet()
    for b in range(BLOCKS):
        total.near(b).start()
    pert_copy.start()
    for b in range(BLOCKS):
        total.second(b)
    exchange.start()
    pert_copy.wait()

    def block(b, start, count):
        fine_adj = full_ref[8 * b:8 * b + 8]

        def member(k, carry):
            fine = fine_adj * pert_ref[k, 8 * b:8 * b + 8].astype(F32)
            hi, lo = split(fine.reshape(256, 128))
            turn_ref[pl.ds(k * 32 + 8 * b, 8)] = mm(gx_ref[...], jnp.concatenate([hi, lo], 0)).reshape(8, 16, 128)
            return carry

        if count == 4:
            for k in range(4):
                member(start + k, 0)
        else:
            lax.fori_loop(start, start + count, member, 0, unroll=4)

    for s in range(BLOCKS + 1):
        if s < BLOCKS:
            total.third(s, lambda at: 0.0)
        if s >= 1:
            total.last(s - 1)
            if s < BLOCKS:
                block(s - 1, 0, 20)

    mix = mixing(lv_ref[...])

    def smooth(g, carry):
        block(BLOCKS - 1, 4 * g, 4)
        rows = []
        for a in range(9):
            hi, lo = split(turn_ref[pl.ds(pl.multiple_of(g * 128, 128), 128), a, :])
            rows.append(mm(gy_ref[...], jnp.concatenate([hi, lo], 1), NT))
        field = three(jnp.concatenate(rows, 0), mix).reshape(9, 40, 128)
        field = jnp.concatenate([jnp.zeros((9, 8, 128), F32), field], 1)
        for step in range(4):
            two = jnp.zeros((2, 48, 128), F32)
            field = diffuse_rows(jnp.concatenate([two, field, two], 0))
        wide_ref[g] = field
        for copy in y_copies(g):
            copy.start()
        return carry

    def lengthways(g, carry):
        for copy in y_copies(g):
            copy.wait()
        wide_ref[g, :, 8:16] += fromleft_ref[g]
        wide_ref[g, :, 32:40] += fromright_ref[g]
        for copy in x_copies(g):
            copy.start()
        return carry

    def both(g, carry):
        smooth(g, carry)
        return lengthways(g - 1, carry)

    smooth(0, 0)
    lax.fori_loop(1, CHUNKS, both, 0)
    lengthways(CHUNKS - 1, 0)

    exchange.wait()
    unroute(tgt_ref, ret_ref[...].reshape(128, 128), depout_ref)
    for g in range(CHUNKS):
        for copy in x_copies(g):
            copy.wait()
        lanes = slice(128 * g, 128 * g + 128)
        grad_ref[:, :, lanes] = wide_ref[g, 4:12, 8:40]
        grad_ref[0:5, :, lanes] += fromabove_ref[g]
        grad_ref[4:8, :, lanes] += frombelow_ref[g]


def backward(adj, dep, tgt, pert, lv, gy, gx):
    return pl.pallas_call(
        backward_kernel,
        out_shape=(
            jax.ShapeDtypeStruct((8, 32, 640), F32),
            jax.ShapeDtypeStruct((32, 32, 128), F32),
            jax.ShapeDtypeStruct(tgt.shape, F32),
        ),
        in_specs=[VMEM] * 3 + [ANY] + [VMEM] * 3,
        out_specs=(VMEM,) * 3,
        scratch_shapes=[
            pltpu.VMEM(pert.shape, BF16),
            pltpu.VMEM((640, 16, 128), F32),
            pltpu.VMEM((CHUNKS, 17, 48, 128), F32),
            pltpu.VMEM((CHUNKS, 17, 8, 128), F32),
            pltpu.VMEM((CHUNKS, 17, 8, 128), F32),
            pltpu.VMEM((CHUNKS, 5, 32, 128), F32),
            pltpu.VMEM((CHUNKS, 4, 32, 128), F32),
            pltpu.VMEM((GROUPS, 4, 128), F32),
        ] + MEM_SCRATCH + [DMA((2, CHUNKS))] * 4 + [DMA((GROUPS,))] * 2 + [DMA((2,))],
        compiler_params=pltpu.CompilerParams(vmem_limit_bytes=VMEM_LIMIT, collective_id=1, has_side_effects=True),
        name="backward",
    )(adj, dep, tgt, pert, lv, gy, gx)


def finish_kernel(alpha_ref, back_ref, bg_ref, static_ref, adj_ref, dep_ref, grad_ref, gstat_ref, out_ref):
    grad_ref[...] = alpha_ref[...] + back_ref[...]
    gstat_ref[...] = static_ref[...] + bg_ref[...] * adj_ref[...]
    out_ref[...] = dep_ref[...]


def finish(alpha, back, bg, static, adj, dep):
    return pl.pallas_call(
        finish_kernel,
        out_shape=tuple(jax.ShapeDtypeStruct(a.shape, F32) for a in (alpha, static, dep)),
        in_specs=[VMEM] * 6,
        out_specs=(VMEM,) * 3,
        compiler_params=pltpu.CompilerParams(vmem_limit_bytes=VMEM_LIMIT),
        name="finish",
    )(alpha, back, bg, static, adj, dep)


def per_device(alpha, lv_sqrt, ens_pert, bg_sigma, static_ctrl, obs_owner, obs_column, obs_level, obs_frac, innovation, obs_rinv, obs_count):
    spread_y, gather_y, spread_x, gather_x = tables()
    shape = (64, 128)
    table, incoming, order, target = forward(
        obs_count, obs_owner.reshape(shape), obs_column.reshape(shape), obs_level.reshape(shape), obs_frac,
        innovation.reshape(shape), obs_rinv.reshape(shape), alpha, ens_pert, bg_sigma, static_ctrl, lv_sqrt, spread_y, spread_x,
    )
    departure, adjoint = stencil(order, table, incoming)
    back, adjoint, departures = backward(adjoint.reshape(32, 32, 128), departure, target, ens_pert, lv_sqrt, gather_y, gather_x)
    grad_alpha, grad_static, departures = finish(alpha, back, bg_sigma, static_ctrl, adjoint, departures)
    return grad_alpha, grad_static, departures.reshape(-1)


def solution(mesh):
    placed = (
        P("tx", "ty", "mem"),
        P(),
        P("mem", None, "tx", "ty"),
        P(None, "tx", "ty"),
        P(None, "tx", "ty"),
        P(("tx", "ty", "mem"), None),
        P(("tx", "ty", "mem")),
        P(("tx", "ty", "mem")),
        P(None, ("tx", "ty", "mem")),
        P(("tx", "ty", "mem")),
        P(("tx", "ty", "mem")),
        P(("tx", "ty", "mem")),
    )
    return jax.shard_map(
        per_device,
        mesh=mesh,
        in_specs=placed,
        out_specs=(P("tx", "ty", "mem"), P(None, "tx", "ty"), P(("tx", "ty", "mem"))),
        check_vma=False,
    )
```

```python
import functools
import numpy as np
import jax
import jax.numpy as jnp
from jax import lax
from jax.experimental import pallas as pl
from jax.experimental.pallas import tpu as pltpu
from jax.sharding import PartitionSpec as P

F32 = jnp.float32
BF16 = jnp.bfloat16
NU = 0.2
RATIO = 4
VMEM_LIMIT = 56 * 1024 * 1024
NN = (((1,), (0,)), ((), ()))
NT = (((1,), (1,)), ((), ()))
TN = (((0,), (0,)), ((), ()))


def mm(a, b, dims=NN):
    return lax.dot_general(a, b, dims, preferred_element_type=F32)


def split(v):
    hi = v.astype(BF16)
    return hi, (v - hi.astype(F32)).astype(BF16)


def iota(shape, dim):
    return lax.broadcasted_iota(jnp.int32, shape, dim)


def tent(position, count):
    return jnp.maximum(1.0 - jnp.abs(position - iota((count, 128), 0).astype(F32)), 0.0)


def chunk_order(obs_ref):
    base = obs_ref[:, 20:24, :].astype(jnp.int32)
    live = obs_ref[:, 16:20, :] > 0.0
    level = base // 4096
    first = jnp.min(jnp.where(live, level, 99), 2, keepdims=True).astype(F32)
    last = jnp.max(jnp.where(live, level + 1, -1), 2, keepdims=True).astype(F32)
    spread = lambda v: jnp.broadcast_to(v, (32, 4, 128)).reshape(128, 128)
    first, last = spread(first), spread(last)
    down, along = iota((128, 128), 0), iota((128, 128), 1)
    key = first * 16384.0 + last * 128.0 + down.astype(F32)
    other = key.T
    rank = jnp.sum(jnp.where(other > key, 1.0, 0.0), 0, keepdims=True)
    hit = along == jnp.broadcast_to(rank, (128, 128)).T.astype(jnp.int32)
    pick = lambda v: jnp.sum(jnp.where(hit, v, 0.0), 0, keepdims=True)
    live_count = jnp.sum(jnp.where(other < 98.0 * 16384.0, 1.0, 0.0), 1, keepdims=True)
    count = jnp.broadcast_to(live_count, (128, 128))[0:1]
    rows = [pick(down.astype(F32)), pick(first), pick(last), count]
    return jnp.concatenate(rows + [jnp.zeros((4, 128), F32)], 0).astype(jnp.int32)


def stencil_kernel(order_ref, table_ref, obs_ref, dep_ref, adj_ref, acc_ref, ahi0, alo0, ahi1, alo1, place_ref, in_x_ref, in_y_ref, sum_ref, spread_ref, where_ref):
    slots = ((ahi0, alo0), (ahi1, alo1))
    acc_ref[...] = jnp.zeros_like(acc_ref)
    dep_ref[...] = jnp.zeros_like(dep_ref)
    ahi1[0:512] = jnp.zeros((512, 512), BF16)
    alo1[0:512] = jnp.zeros((512, 512), BF16)
    base = obs_ref[:, 20:24, :].astype(jnp.int32)
    where_ref[:, 0:4] = (base >> 12).astype(F32) + obs_ref[:, 8:12, :]
    where_ref[:, 4:8] = ((base >> 7) & 31).astype(F32) + obs_ref[:, 0:4, :]
    where_ref[:, 8:12] = (base & 127).astype(F32) + obs_ref[:, 4:8, :]
    spread_ref[...] = jnp.zeros_like(spread_ref)
    groups = (order_ref[3, 0] + 3) // 4

    def lanes(start, step, wide):
        return pl.ds(pl.multiple_of((start + step) * 128, 128), wide)

    def adjoint(slot, at, rows):
        acc_ref[0:256, at] += mm(spread_ref[...], slots[slot][0][rows], NT)
        acc_ref[256:384, at] += mm(spread_ref[0:128], slots[slot][1][rows], NT)

    def more(start, rest, what):
        def one(g, carry):
            what(lanes(start, 4 + 2 * g, 256), pl.ds(pl.multiple_of(512 + 256 * g, 256), 256), 16 + 8 * g)
            return carry

        lax.fori_loop(0, rest, one, 0)

    def one_group(n, slot, before):
        ahi_ref, alo_ref = slots[slot]
        old_start, old_rest = before
        first_of = jnp.minimum(4 * n, 124)
        first = order_ref[1, first_of]
        last = order_ref[2, first_of]
        for j in range(1, 4):
            first = jnp.minimum(first, order_ref[1, first_of + j])
            last = jnp.maximum(last, order_ref[2, first_of + j])
        start = jnp.minimum(first // 4, 4)
        rest = jnp.maximum(last - 4 * start - 16 + 8, 0) // 8
        rest = jnp.where(n < groups, rest, 0)

        adjoint(1 - slot, lanes(old_start, 0, 512), slice(0, 512))
        sources, parts = [], []
        for j in range(4):
            chunk = order_ref[0, first_of + j]
            s, q = chunk // 4, lax.rem(chunk, 4)
            sources.append(s)
            parts.append(q)
            get = lambda ch: where_ref[s, pl.ds(ch * 4 + q, 1), :]
            at = slice(128 * j, 128 * j + 128)
            place_ref[:, at] = jnp.broadcast_to(get(0) - (4 * start).astype(F32), (8, 128))
            in_x_ref[:, at] = tent(get(1), 32)
            in_y_ref[:, at] = tent(get(2), 128)

        def build(row, level):
            far = place_ref[...] - (iota((8, 512), 0) + level).astype(F32)
            in_l = jnp.maximum(1.0 - jnp.abs(far), 0.0)
            for l in range(8):
                hi, lo = split(in_l[l:l + 1] * in_x_ref[...])
                at = pl.ds(row + 32 * l, 32)
                ahi_ref[at] = hi
                alo_ref[at] = lo

        build(0, 0)
        build(256, 8)
        table = table_ref[:, lanes(start, 0, 512)]
        both = mm(table, ahi_ref[0:512])
        sum_ref[...] = both[:128] + both[128:] + mm(table[:128], alo_ref[0:512])

        def gather(at, rows, level):
            build(pl.multiple_of(32 * level, 256), level)
            table = table_ref[:, at]
            both = mm(table, ahi_ref[rows])
            sum_ref[...] += both[:128] + both[128:] + mm(table[:128], alo_ref[rows])

        more(old_start, old_rest, lambda at, rows, level: adjoint(1 - slot, at, rows))
        more(start, rest, gather)

        for j in range(4):
            at = slice(128 * j, 128 * j + 128)
            get = lambda ch: obs_ref[sources[j], pl.ds(ch * 4 + parts[j], 1), :]
            dep = jnp.sum(sum_ref[:, at] * in_y_ref[:, at], 0, keepdims=True) - get(3)
            dep_ref[sources[j], pl.ds(parts[j], 1), :] = dep
            hi, lo = split(in_y_ref[:, at] * (dep * get(4)))
            spread_ref[0:128, at] = hi
            spread_ref[128:256, at] = lo
        return start, rest

    def two_groups(i, before):
        return one_group(2 * i + 1, 1, one_group(2 * i, 0, before))

    start, rest = lax.fori_loop(0, (groups + 1) // 2, two_groups, (jnp.int32(0), jnp.int32(0)))
    adjoint(1, lanes(start, 0, 512), slice(0, 512))
    more(start, rest, lambda at, rows, level: adjoint(1, at, rows))
    adj_ref[...] = (acc_ref[0:128, 0:1024] + acc_ref[128:256, 0:1024] + acc_ref[256:384, 0:1024]).T


def stencil(order, table, obs):
    return pl.pallas_call(
        stencil_kernel,
        out_shape=(jax.ShapeDtypeStruct((32, 4, 128), F32), jax.ShapeDtypeStruct((1024, 128), F32)),
        in_specs=[pl.BlockSpec(memory_space=pltpu.SMEM)] + [pl.BlockSpec(memory_space=pltpu.VMEM)] * 2,
        out_specs=(pl.BlockSpec(memory_space=pltpu.VMEM),) * 2,
        scratch_shapes=[
            pltpu.VMEM((384, 1280), F32),
            pltpu.VMEM((1280, 512), BF16),
            pltpu.VMEM((1280, 512), BF16),
            pltpu.VMEM((1280, 512), BF16),
            pltpu.VMEM((1280, 512), BF16),
            pltpu.VMEM((8, 512), F32),
            pltpu.VMEM((32, 512), F32),
            pltpu.VMEM((128, 512), F32),
            pltpu.VMEM((128, 512), F32),
            pltpu.VMEM((256, 512), BF16),
            pltpu.VMEM((32, 16, 128), F32),
        ],
        compiler_params=pltpu.CompilerParams(vmem_limit_bytes=VMEM_LIMIT),
        name="stencil",
    )(order, table, obs)


def line_weights(fine, coarse):
    out = np.zeros((fine, coarse), np.float32)
    for f in range(fine):
        out[f, f // RATIO] += 1.0 - (f % RATIO) / RATIO
        out[f, f // RATIO + 1] += (f % RATIO) / RATIO
    return out


def tables():
    along = line_weights(128, 40)
    across = line_weights(32, 16)
    spread_y = np.concatenate([along.T, along.T], 0)
    gather_y = np.concatenate([along.T, along.T], 1)
    eye = np.eye(8, dtype=np.float32)
    block = np.kron(eye, across)
    spread_x = np.concatenate([block, block], 1)
    gather_x = np.concatenate([block.T, block.T], 1)
    return [jnp.asarray(t, BF16) for t in (spread_y, gather_y, spread_x, gather_x)]


def diffuse_rows(field, first, last):
    near = field[first - 1:last - 1] + field[first + 1:last + 1]
    mid = field[first:last]
    near = near + pltpu.roll(mid, 1, 1) + pltpu.roll(mid, 47, 1)
    return mid + NU * (near - 4.0 * mid)


def three(a, b_ref):
    hi, lo = split(a)
    return mm(jnp.concatenate([hi, lo, hi], 1), b_ref[...])

MESH = pl.DeviceIdType.MESH
GROUPS = 32
CHUNKS = 5
BLOCKS = 4


def tile_id(index, mem):
    return (index // 4, index % 4, mem)


def remote(src, dst, send, recv, device):
    return pltpu.make_async_remote_copy(src_ref=src, dst_ref=dst, send_sem=send, recv_sem=recv, device_id=device, device_id_type=MESH)


class Place:
    def __init__(self):
        self.tx, self.ty, self.mem = lax.axis_index("tx"), lax.axis_index("ty"), lax.axis_index("mem")
        self.core = self.mem % 2
        self.below = (lax.rem(self.tx + 1, 8), self.ty, self.mem)
        self.above = (lax.rem(self.tx + 7, 8), self.ty, self.mem)
        self.right = (self.tx, lax.rem(self.ty + 1, 4), self.mem)
        self.left = (self.tx, lax.rem(self.ty + 3, 4), self.mem)
        self.twin = (self.tx, self.ty, self.mem + 1 - 2 * self.core)
        self.across = (self.tx, self.ty, lax.rem(self.mem + 2, 4))

    def along_ty(self, d):
        return (self.tx, lax.rem(self.ty + d, 4), self.mem)

    def along_tx(self, d):
        return (lax.rem(self.tx + d, 8), self.ty, self.mem)

    def greet(self):
        barrier = pltpu.get_barrier_semaphore()
        others = [self.along_tx(d) for d in range(1, 8)] + [self.along_ty(d) for d in range(1, 4)] + [self.twin, self.across]
        for other in others:
            pl.semaphore_signal(barrier, inc=1, device_id=other, device_id_type=MESH)
        pl.semaphore_wait(barrier, len(others))


class Exchange:
    def __init__(self, place, src, mid, dst, send, recv, own):
        self.place, self.src, self.mid, self.dst, self.send, self.recv, self.own = place, src, mid, dst, send, recv, own

    def first(self, d):
        other = self.place.along_ty(d)
        return remote(self.src.at[:, other[1]], self.mid.at[self.place.ty], self.send.at[d - 1], self.recv.at[d - 1], other)

    def second(self, d):
        other = self.place.along_tx(d)
        return remote(self.mid.at[:, other[0]], self.dst.at[self.place.tx], self.send.at[d + 2], self.recv.at[d + 2], other)

    def keep(self, at):
        if at == 0:
            return pltpu.make_async_copy(self.src.at[:, self.place.ty], self.mid.at[self.place.ty], self.own.at[0])
        return pltpu.make_async_copy(self.mid.at[:, self.place.tx], self.dst.at[self.place.tx], self.own.at[1])

    def start(self):
        self.keep(0).start()
        for d in range(1, 4):
            self.first(d).start()

    def turn(self):
        self.keep(0).wait()
        for d in range(1, 4):
            self.first(d).wait()
        self.keep(1).start()
        for d in range(1, 8):
            self.second(d).start()

    def wait(self):
        self.keep(1).wait()
        for d in range(1, 8):
            self.second(d).wait()


class MemSum:
    def __init__(self, place, part, total, half, got, far, send, recv):
        self.place, self.part, self.total = place, part, total
        self.half, self.got, self.far, self.send, self.recv = half, got, far, send, recv

    def mine(self, b):
        return pl.ds(8 * b + 4 * self.place.core, 4)

    def near(self, b):
        return remote(self.part.at[pl.ds(8 * b + 4 - 4 * self.place.core, 4)], self.got.at[b], self.send.at[0, b], self.recv.at[0, b], self.place.twin)

    def over(self, b):
        return remote(self.half.at[b], self.far.at[b], self.send.at[1, b], self.recv.at[1, b], self.place.across)

    def back(self, b):
        return remote(self.total.at[self.mine(b)], self.total.at[self.mine(b)], self.send.at[2, b], self.recv.at[2, b], self.place.twin)

    def second(self, b):
        self.near(b).wait()
        self.half[b] = self.part[self.mine(b)] + self.got[b]
        self.over(b).start()

    def third(self, b, extra):
        self.over(b).wait()
        self.total[self.mine(b)] = self.half[b] + self.far[b] + extra(self.mine(b))
        self.back(b).start()

    def last(self, b):
        self.back(b).wait()


MEM_SCRATCH = [pltpu.VMEM((BLOCKS, 4, 32, 128), F32)] * 3 + [pltpu.SemaphoreType.DMA((3, BLOCKS))] * 2


def route_ranks(cnt_ref, owner_ref, col_ref, lev_ref, frac_ref, inn_ref, rinv_ref, tgt_ref, high_ref, low_ref, term_ref):
    rows, wide = owner_ref.shape
    place = iota((rows, wide), 0) * wide + iota((rows, wide), 1)
    live = place < cnt_ref[0]
    owner = jnp.where(live, owner_ref[...], GROUPS)
    level = lev_ref[...]
    key = (owner * 32 + level).astype(F32)
    turned = jnp.concatenate([key, key], 0).T
    earlier = iota((wide, wide), 0) < iota((wide, wide), 1)
    one_if = lambda cond: jnp.where(cond, 1.0, 0.0).astype(BF16)
    owners = [one_if(iota((GROUPS, wide), 0) == owner[c:c + 1]) for c in range(rows)]
    levels = [one_if(iota((32, wide), 0) == level[c:c + 1]) for c in range(rows)]
    running = jnp.zeros((GROUPS, 32), F32)
    starts = []
    for c in range(rows):
        starts.append(running)
        running = running + mm(owners[c], levels[c], NT)
    lower = one_if(iota((32, 32), 0) < iota((32, 32), 1))
    hi, lo = split(running)
    offset = mm(hi, lower) + mm(lo, lower)
    ranks = []
    for c in range(rows):
        hi, lo = split(offset + starts[c])
        both = mm(jnp.concatenate([hi, lo], 0), levels[c])
        same = jnp.where((turned[:, c:c + 1] == key[c:c + 1]) & earlier, 1.0, 0.0)
        at = (both[:GROUPS] + both[GROUPS:]) * owners[c].astype(F32)
        ranks.append(jnp.sum(at, 0, keepdims=True) + jnp.sum(same, 0, keepdims=True))
    rank = jnp.where(live, jnp.concatenate(ranks, 0).astype(jnp.int32), 0)
    tgt_ref[...] = jnp.where(live, owner * 512 + rank, -1)
    high_ref[...] = jnp.where(live, rank // 128 * GROUPS + owner, -1)
    low_ref[...] = rank % 128
    base = (lev_ref[...] * 4096 + col_ref[...]).astype(F32)
    for at, v in ((3, inn_ref[...]), (4, rinv_ref[...]), (5, base)):
        hi, lo = split(v)
        term_ref[2 * at] = hi.astype(F32)
        term_ref[2 * at + 1] = lo.astype(F32)
    for at in range(3):
        for r in range(rows):
            hi, lo = split(frac_ref[at:at + 1, wide * r:wide * (r + 1)])
            term_ref[2 * at, r:r + 1] = hi.astype(F32)
            term_ref[2 * at + 1, r:r + 1] = lo.astype(F32)


def route_slots(start, count, high_ref, low_ref, term_ref, acc_ref):
    def one(c, carry):
        def line(ref, *at):
            rows = ref[(*at, pl.ds(pl.multiple_of(8 * c, 8), 8), slice(None))]
            return jnp.concatenate([rows[r:r + 1] for r in range(8)], 1)

        hit = jnp.where(iota((128, 1024), 0) == line(high_ref), 1.0, 0.0).astype(BF16)
        lane = jnp.where(iota((128, 1024), 0) == line(low_ref), 1.0, 0.0).astype(BF16)
        for ch in range(6):
            stack = jnp.concatenate([lane * line(term_ref, 2 * ch + t).astype(BF16) for t in range(2)], 0)
            acc_ref[:, 256 * ch:256 * ch + 256] += mm(hit, stack, NT)
        return carry

    lax.fori_loop(start, start + count, one, 0)


def route_out(acc_ref, out_ref):
    for ch in range(6):
        full = acc_ref[:, 256 * ch:256 * ch + 128] + acc_ref[:, 256 * ch + 128:256 * ch + 256]
        for q in range(4):
            rows = full[q * GROUPS:(q + 1) * GROUPS].reshape(8, 4, 128)
            out_ref[:, :, ch * 4 + q, :] = rows


def unroute(tgt_ref, ret, out_ref):
    rows = tgt_ref.shape[0]
    hi, lo = split(ret.T)
    table = jnp.concatenate([hi, lo], 0)
    for c in range(0, rows, 2):
        tgt = jnp.concatenate([tgt_ref[c:c + 1], tgt_ref[c + 1:c + 2]], 1)
        hit = jnp.where(iota((128, 256), 0) == tgt // 128, 1.0, 0.0).astype(BF16)
        picked = mm(table, hit)
        picked = picked[:128] + picked[128:]
        row = jnp.sum(jnp.where((iota((128, 256), 0) == tgt % 128) & (tgt >= 0), picked, 0.0), 0, keepdims=True)
        out_ref[c:c + 1] = row[:, :128]
        out_ref[c + 1:c + 2] = row[:, 128:]


def diffuse_rows(field):
    near = field[:-2] + field[2:]
    mid = field[1:-1]
    near = near + pltpu.roll(mid, 1, 1) + pltpu.roll(mid, 47, 1)
    return mid + NU * (near - 4.0 * mid)


def mixing(lv):
    tiled = jnp.concatenate([jnp.concatenate([lv] * 4, 1)] * 4, 0)
    return jnp.where(iota((128, 128), 0) // 32 == iota((128, 128), 1) // 32, tiled, 0.0)


def three(a, b):
    hi, lo = split(a)
    bhi, blo = split(b)
    return mm(jnp.concatenate([hi, lo, hi], 1), jnp.concatenate([bhi, bhi, blo], 0))


def forward_kernel(
    cnt_ref, owner_ref, col_ref, lev_ref, frac_ref, inn_ref, rinv_ref, alpha_ref, pert_hbm, bg_ref, static_ref, lv_ref, sy_ref, sx_ref,
    table_ref, obs_ref, order_ref, tgt_ref,
    inc_ref, halo_ref, fromleft_ref, fromright_ref, mine_ref, pert_ref, turn_ref, part_ref, out_ref, mid_ref, high_ref, low_ref, term_ref, acc_ref,
    half_ref, got_ref, far_ref, msend, mrecv,
    xsend, xrecv, ysend, yrecv, osend, orecv, around, own,
):
    place = Place()

    def x_copies(g):
        lanes = pl.ds(pl.multiple_of(g * 128, 128), 128)
        return (
            remote(alpha_ref.at[4:8, :, lanes], halo_ref.at[g, 0:4, 8:40], xsend.at[0, g], xrecv.at[0, g], place.below),
            remote(alpha_ref.at[0:5, :, lanes], halo_ref.at[g, 4:9, 8:40], xsend.at[1, g], xrecv.at[1, g], place.above),
        )

    y_copies = (
        remote(alpha_ref.at[:, 24:32], fromleft_ref, ysend.at[0, CHUNKS], yrecv.at[0, CHUNKS], place.right),
        remote(alpha_ref.at[:, 0:8], fromright_ref, ysend.at[1, CHUNKS], yrecv.at[1, CHUNKS], place.left),
    )

    def corner_copies(g):
        return (
            remote(halo_ref.at[g, :, 32:40], halo_ref.at[g, :, 0:8], ysend.at[0, g], yrecv.at[0, g], place.right),
            remote(halo_ref.at[g, :, 8:16], halo_ref.at[g, :, 40:48], ysend.at[1, g], yrecv.at[1, g], place.left),
        )

    own_copy = pltpu.make_async_copy(alpha_ref, mine_ref, own.at[0])
    pert_copy = pltpu.make_async_copy(pert_hbm, pert_ref, own.at[1])
    exchange = Exchange(place, out_ref, mid_ref, obs_ref, osend, orecv, around)
    total = MemSum(place, part_ref, inc_ref, half_ref, got_ref, far_ref, msend, mrecv)

    place.greet()

    def begin(g, carry):
        for copy in x_copies(g):
            copy.start()
        return carry

    lax.fori_loop(0, CHUNKS, begin, 0)
    for copy in y_copies:
        copy.start()
    own_copy.start()
    pert_copy.start()
    turn_ref[...] = jnp.zeros_like(turn_ref)
    route_ranks(cnt_ref, owner_ref, col_ref, lev_ref, frac_ref, inn_ref, rinv_ref, tgt_ref, high_ref, low_ref, term_ref)
    acc_ref[...] = jnp.zeros_like(acc_ref)
    mix = mixing(lv_ref[...]).T
    part_ref[...] = jnp.zeros_like(part_ref)
    own_copy.wait()
    pert_copy.wait()
    for copy in y_copies:
        copy.wait()

    def sideways(g):
        for copy in x_copies(g):
            copy.wait()
        for copy in corner_copies(g):
            copy.start()

    def smooth(g):
        for copy in corner_copies(g):
            copy.wait()
        lanes = pl.ds(pl.multiple_of(g * 128, 128), 128)
        center = jnp.concatenate([fromleft_ref[:, :, lanes], mine_ref[:, :, lanes], fromright_ref[:, :, lanes]], 1)
        field = jnp.concatenate([halo_ref[g, 0:4], center, halo_ref[g, 4:9]], 0)
        for step in range(4):
            field = diffuse_rows(field)
        field = three(field[:, 8:48].reshape(9 * 40, 128), mix).reshape(9, 40, 128)
        for a in range(9):
            hi, lo = split(field[a])
            turn_ref[:, a, :] = mm(jnp.concatenate([hi, lo], 0), sy_ref[...], TN)
        for b in range(BLOCKS):
            at = slice(8 * b, 8 * b + 8)
            sums = part_ref[at]
            for k in range(4):
                hi, lo = split(turn_ref[32 * k + 8 * b:32 * k + 8 * b + 8].reshape(128, 128))
                fine = mm(sx_ref[...], jnp.concatenate([hi, lo], 0)).reshape(8, 32, 128)
                sums = sums + fine * pert_ref[4 * g + k, at].astype(F32)
            part_ref[at] = sums

    sideways(0)
    route_slots(0, 4, high_ref, low_ref, term_ref, acc_ref)
    sideways(1)
    route_slots(4, 4, high_ref, low_ref, term_ref, acc_ref)
    sideways(2)
    route_out(acc_ref, out_ref)
    exchange.start()

    def both(g, carry):
        @pl.when(g == 2)
        def _():
            exchange.turn()

        smooth(g)

        @pl.when(g < CHUNKS - 3)
        def _():
            sideways(g + 3)

        return carry

    lax.fori_loop(0, CHUNKS, both, 0)

    extra = lambda at: bg_ref[at] * static_ref[at]
    for b in range(BLOCKS):
        total.near(b).start()
    for b in range(BLOCKS):
        total.second(b)
    exchange.wait()
    order_ref[...] = chunk_order(obs_ref[...].reshape(GROUPS, 24, 128))
    for b in range(BLOCKS):
        total.third(b, extra)
    for b in range(BLOCKS):
        total.last(b)
        hi, lo = split(inc_ref[8 * b:8 * b + 8].reshape(256, 128).T)
        table_ref[0:128, 256 * b:256 * b + 256] = hi
        table_ref[128:256, 256 * b:256 * b + 256] = lo
    table_ref[:, 1024:1280] = jnp.zeros((256, 256), BF16)


VMEM = pl.BlockSpec(memory_space=pltpu.VMEM)
SMEM = pl.BlockSpec(memory_space=pltpu.SMEM)
ANY = pl.BlockSpec(memory_space=pl.ANY)
DMA = pltpu.SemaphoreType.DMA


def forward(cnt, owner, col, lev, frac, inn, rinv, alpha, pert, bg, static, lv, sy, sx):
    return pl.pallas_call(
        forward_kernel,
        out_shape=(
            jax.ShapeDtypeStruct((256, 1280), BF16),
            jax.ShapeDtypeStruct((8, 4, 24, 128), F32),
            jax.ShapeDtypeStruct((8, 128), jnp.int32),
            jax.ShapeDtypeStruct((64, 128), jnp.int32),
        ),
        in_specs=[SMEM] + [VMEM] * 6 + [ANY] * 2 + [VMEM] * 5,
        out_specs=(VMEM,) * 4,
        scratch_shapes=[
            pltpu.VMEM((32, 32, 128), F32),
            pltpu.VMEM((CHUNKS, 9, 48, 128), F32),
            pltpu.VMEM((8, 8, 640), F32),
            pltpu.VMEM((8, 8, 640), F32),
            pltpu.VMEM((8, 32, 640), F32),
            pltpu.VMEM(pert.shape, BF16),
            pltpu.VMEM((128, 16, 128), F32),
            pltpu.VMEM((32, 32, 128), F32),
            pltpu.VMEM((8, 4, 24, 128), F32),
            pltpu.VMEM((4, 8, 24, 128), F32),
            pltpu.VMEM((64, 128), jnp.int32),
            pltpu.VMEM((64, 128), jnp.int32),
            pltpu.VMEM((12, 64, 128), F32),
            pltpu.VMEM((128, 1536), F32),
        ] + MEM_SCRATCH + [DMA((2, CHUNKS))] * 2 + [DMA((2, CHUNKS + 1))] * 2 + [DMA((10,))] * 2 + [DMA((2,)), DMA((2,))],
        compiler_params=pltpu.CompilerParams(vmem_limit_bytes=VMEM_LIMIT, collective_id=0, has_side_effects=True),
        name="forward",
    )(cnt, owner, col, lev, frac, inn, rinv, alpha, pert, bg, static, lv, sy, sx)


def backward_kernel(
    adj_ref, dep_ref, tgt_ref, pert_hbm, lv_ref, gy_ref, gx_ref,
    grad_ref, full_ref, depout_ref,
    pert_ref, turn_ref, wide_ref, fromleft_ref, fromright_ref, fromabove_ref, frombelow_ref, mid_ref, ret_ref,
    half_ref, got_ref, far_ref, msend, mrecv,
    xsend, xrecv, ysend, yrecv, osend, orecv, around, own,
):
    place = Place()

    def y_copies(g):
        return (
            remote(wide_ref.at[g, :, 40:48], fromleft_ref.at[g], ysend.at[0, g], yrecv.at[0, g], place.right),
            remote(wide_ref.at[g, :, 0:8], fromright_ref.at[g], ysend.at[1, g], yrecv.at[1, g], place.left),
        )

    def x_copies(g):
        return (
            remote(wide_ref.at[g, 12:17, 8:40], fromabove_ref.at[g], xsend.at[0, g], xrecv.at[0, g], place.below),
            remote(wide_ref.at[g, 0:4, 8:40], frombelow_ref.at[g], xsend.at[1, g], xrecv.at[1, g], place.above),
        )

    pert_copy = pltpu.make_async_copy(pert_hbm, pert_ref, own.at[0])
    exchange = Exchange(place, dep_ref, mid_ref, ret_ref, osend, orecv, around)
    total = MemSum(place, adj_ref, full_ref, half_ref, got_ref, far_ref, msend, mrecv)

    place.greet()
    for b in range(BLOCKS):
        total.near(b).start()
    pert_copy.start()
    for b in range(BLOCKS):
        total.second(b)
    exchange.start()
    pert_copy.wait()

    def block(b, start, count):
        fine_adj = full_ref[8 * b:8 * b + 8]

        def member(k, carry):
            fine = fine_adj * pert_ref[k, 8 * b:8 * b + 8].astype(F32)
            hi, lo = split(fine.reshape(256, 128))
            turn_ref[pl.ds(k * 32 + 8 * b, 8)] = mm(gx_ref[...], jnp.concatenate([hi, lo], 0)).reshape(8, 16, 128)
            return carry

        if count == 4:
            for k in range(4):
                member(start + k, 0)
        else:
            lax.fori_loop(start, start + count, member, 0, unroll=4)

    for s in range(BLOCKS + 1):
        if s < BLOCKS:
            total.third(s, lambda at: 0.0)
        if s >= 1:
            total.last(s - 1)
            if s < BLOCKS:
                block(s - 1, 0, 20)

    exchange.turn()
    mix = mixing(lv_ref[...])

    def smooth(g, carry):
        block(BLOCKS - 1, 4 * g, 4)
        rows = []
        for a in range(9):
            hi, lo = split(turn_ref[pl.ds(pl.multiple_of(g * 128, 128), 128), a, :])
            rows.append(mm(gy_ref[...], jnp.concatenate([hi, lo], 1), NT))
        field = three(jnp.concatenate(rows, 0), mix).reshape(9, 40, 128)
        field = jnp.concatenate([jnp.zeros((9, 8, 128), F32), field], 1)
        for step in range(4):
            two = jnp.zeros((2, 48, 128), F32)
            field = diffuse_rows(jnp.concatenate([two, field, two], 0))
        wide_ref[g] = field
        for copy in y_copies(g):
            copy.start()
        return carry

    def lengthways(g, carry):
        for copy in y_copies(g):
            copy.wait()
        wide_ref[g, :, 8:16] += fromleft_ref[g]
        wide_ref[g, :, 32:40] += fromright_ref[g]
        for copy in x_copies(g):
            copy.start()
        return carry

    def both(g, carry):
        smooth(g, carry)
        return lengthways(g - 1, carry)

    smooth(0, 0)
    lax.fori_loop(1, CHUNKS, both, 0)
    lengthways(CHUNKS - 1, 0)

    exchange.wait()
    unroute(tgt_ref, ret_ref[...].reshape(128, 128), depout_ref)
    for g in range(CHUNKS):
        for copy in x_copies(g):
            copy.wait()
        lanes = slice(128 * g, 128 * g + 128)
        grad_ref[:, :, lanes] = wide_ref[g, 4:12, 8:40]
        grad_ref[0:5, :, lanes] += fromabove_ref[g]
        grad_ref[4:8, :, lanes] += frombelow_ref[g]


def backward(adj, dep, tgt, pert, lv, gy, gx):
    return pl.pallas_call(
        backward_kernel,
        out_shape=(
            jax.ShapeDtypeStruct((8, 32, 640), F32),
            jax.ShapeDtypeStruct((32, 32, 128), F32),
            jax.ShapeDtypeStruct(tgt.shape, F32),
        ),
        in_specs=[VMEM] * 3 + [ANY] + [VMEM] * 3,
        out_specs=(VMEM,) * 3,
        scratch_shapes=[
            pltpu.VMEM(pert.shape, BF16),
            pltpu.VMEM((640, 16, 128), F32),
            pltpu.VMEM((CHUNKS, 17, 48, 128), F32),
            pltpu.VMEM((CHUNKS, 17, 8, 128), F32),
            pltpu.VMEM((CHUNKS, 17, 8, 128), F32),
            pltpu.VMEM((CHUNKS, 5, 32, 128), F32),
            pltpu.VMEM((CHUNKS, 4, 32, 128), F32),
            pltpu.VMEM((4, 8, 4, 128), F32),
            pltpu.VMEM((8, 4, 4, 128), F32),
        ] + MEM_SCRATCH + [DMA((2, CHUNKS))] * 4 + [DMA((10,))] * 2 + [DMA((2,)), DMA((1,))],
        compiler_params=pltpu.CompilerParams(vmem_limit_bytes=VMEM_LIMIT, collective_id=1, has_side_effects=True),
        name="backward",
    )(adj, dep, tgt, pert, lv, gy, gx)


def finish_kernel(alpha_ref, back_ref, bg_ref, static_ref, adj_ref, dep_ref, grad_ref, gstat_ref, out_ref):
    grad_ref[...] = alpha_ref[...] + back_ref[...]
    gstat_ref[...] = static_ref[...] + bg_ref[...] * adj_ref[...]
    out_ref[...] = dep_ref[...]


def finish(alpha, back, bg, static, adj, dep):
    return pl.pallas_call(
        finish_kernel,
        out_shape=tuple(jax.ShapeDtypeStruct(a.shape, F32) for a in (alpha, static, dep)),
        in_specs=[VMEM] * 6,
        out_specs=(VMEM,) * 3,
        compiler_params=pltpu.CompilerParams(vmem_limit_bytes=VMEM_LIMIT),
        name="finish",
    )(alpha, back, bg, static, adj, dep)


def per_device(alpha, lv_sqrt, ens_pert, bg_sigma, static_ctrl, obs_owner, obs_column, obs_level, obs_frac, innovation, obs_rinv, obs_count):
    spread_y, gather_y, spread_x, gather_x = tables()
    shape = (64, 128)
    table, incoming, order, target = forward(
        obs_count, obs_owner.reshape(shape), obs_column.reshape(shape), obs_level.reshape(shape), obs_frac,
        innovation.reshape(shape), obs_rinv.reshape(shape), alpha, ens_pert, bg_sigma, static_ctrl, lv_sqrt, spread_y, spread_x,
    )
    departure, adjoint = stencil(order, table, incoming.reshape(GROUPS, 24, 128))
    back, adjoint, departures = backward(adjoint.reshape(32, 32, 128), departure.reshape(8, 4, 4, 128), target, ens_pert, lv_sqrt, gather_y, gather_x)
    grad_alpha, grad_static, departures = finish(alpha, back, bg_sigma, static_ctrl, adjoint, departures)
    return grad_alpha, grad_static, departures.reshape(-1)


def solution(mesh):
    placed = (
        P("tx", "ty", "mem"),
        P(),
        P("mem", None, "tx", "ty"),
        P(None, "tx", "ty"),
        P(None, "tx", "ty"),
        P(("tx", "ty", "mem"), None),
        P(("tx", "ty", "mem")),
        P(("tx", "ty", "mem")),
        P(None, ("tx", "ty", "mem")),
        P(("tx", "ty", "mem")),
        P(("tx", "ty", "mem")),
        P(("tx", "ty", "mem")),
    )
    return jax.shard_map(
        per_device,
        mesh=mesh,
        in_specs=placed,
        out_specs=(P("tx", "ty", "mem"), P(None, "tx", "ty"), P(("tx", "ty", "mem"))),
        check_vma=False,
    )
```

```python
import functools
import numpy as np
import jax
import jax.numpy as jnp
from jax import lax
from jax.experimental import pallas as pl
from jax.experimental.pallas import tpu as pltpu
from jax.sharding import PartitionSpec as P

F32 = jnp.float32
BF16 = jnp.bfloat16
NU = 0.2
RATIO = 4
VMEM_LIMIT = 56 * 1024 * 1024
NN = (((1,), (0,)), ((), ()))
NT = (((1,), (1,)), ((), ()))
TN = (((0,), (0,)), ((), ()))


def mm(a, b, dims=NN):
    return lax.dot_general(a, b, dims, preferred_element_type=F32)


def split(v):
    hi = v.astype(BF16)
    return hi, (v - hi.astype(F32)).astype(BF16)


def iota(shape, dim):
    return lax.broadcasted_iota(jnp.int32, shape, dim)


def tent(position, count):
    return jnp.maximum(1.0 - jnp.abs(position - iota((count, 128), 0).astype(F32)), 0.0)


def chunk_order(obs_ref):
    base = obs_ref[:, 20:24, :].astype(jnp.int32)
    live = obs_ref[:, 16:20, :] > 0.0
    level = base // 4096
    first = jnp.min(jnp.where(live, level, 99), 2, keepdims=True).astype(F32)
    last = jnp.max(jnp.where(live, level + 1, -1), 2, keepdims=True).astype(F32)
    spread = lambda v: jnp.broadcast_to(v, (32, 4, 128)).reshape(128, 128)
    first, last = spread(first), spread(last)
    down, along = iota((128, 128), 0), iota((128, 128), 1)
    key = first * 16384.0 + last * 128.0 + down.astype(F32)
    other = key.T
    rank = jnp.sum(jnp.where(other > key, 1.0, 0.0), 0, keepdims=True)
    hit = along == jnp.broadcast_to(rank, (128, 128)).T.astype(jnp.int32)
    pick = lambda v: jnp.sum(jnp.where(hit, v, 0.0), 0, keepdims=True)
    live_count = jnp.sum(jnp.where(other < 98.0 * 16384.0, 1.0, 0.0), 1, keepdims=True)
    count = jnp.broadcast_to(live_count, (128, 128))[0:1]
    rows = [pick(down.astype(F32)), pick(first), pick(last), count]
    return jnp.concatenate(rows + [jnp.zeros((4, 128), F32)], 0).astype(jnp.int32)


def stencil_kernel(order_ref, table_ref, obs_ref, dep_ref, adj_ref, acc_ref, ahi0, alo0, ahi1, alo1, place_ref, in_x_ref, in_y_ref, sum_ref, spread_ref, where_ref):
    slots = ((ahi0, alo0), (ahi1, alo1))
    acc_ref[...] = jnp.zeros_like(acc_ref)
    dep_ref[...] = jnp.zeros_like(dep_ref)
    ahi1[0:512] = jnp.zeros((512, 512), BF16)
    alo1[0:512] = jnp.zeros((512, 512), BF16)
    base = obs_ref[:, 20:24, :].astype(jnp.int32)
    where_ref[:, 0:4] = (base >> 12).astype(F32) + obs_ref[:, 8:12, :]
    where_ref[:, 4:8] = ((base >> 7) & 31).astype(F32) + obs_ref[:, 0:4, :]
    where_ref[:, 8:12] = (base & 127).astype(F32) + obs_ref[:, 4:8, :]
    spread_ref[...] = jnp.zeros_like(spread_ref)
    groups = (order_ref[3, 0] + 3) // 4

    def lanes(start, step, wide):
        return pl.ds(pl.multiple_of((start + step) * 128, 128), wide)

    def adjoint(slot, at, rows):
        acc_ref[0:256, at] += mm(spread_ref[...], slots[slot][0][rows], NT)
        acc_ref[256:384, at] += mm(spread_ref[0:128], slots[slot][1][rows], NT)

    def more(start, rest, what):
        def one(g, carry):
            what(lanes(start, 4 + 2 * g, 256), pl.ds(pl.multiple_of(512 + 256 * g, 256), 256), 16 + 8 * g)
            return carry

        lax.fori_loop(0, rest, one, 0)

    def one_group(n, slot, before):
        ahi_ref, alo_ref = slots[slot]
        old_start, old_rest = before
        first_of = jnp.minimum(4 * n, 124)
        first = order_ref[1, first_of]
        last = order_ref[2, first_of]
        for j in range(1, 4):
            first = jnp.minimum(first, order_ref[1, first_of + j])
            last = jnp.maximum(last, order_ref[2, first_of + j])
        start = jnp.minimum(first // 4, 4)
        rest = jnp.maximum(last - 4 * start - 16 + 8, 0) // 8
        rest = jnp.where(n < groups, rest, 0)

        adjoint(1 - slot, lanes(old_start, 0, 512), slice(0, 512))
        sources, parts = [], []
        for j in range(4):
            chunk = order_ref[0, first_of + j]
            s, q = chunk // 4, lax.rem(chunk, 4)
            sources.append(s)
            parts.append(q)
            get = lambda ch: where_ref[s, pl.ds(ch * 4 + q, 1), :]
            at = slice(128 * j, 128 * j + 128)
            place_ref[:, at] = jnp.broadcast_to(get(0) - (4 * start).astype(F32), (8, 128))
            in_x_ref[:, at] = tent(get(1), 32)
            in_y_ref[:, at] = tent(get(2), 128)

        def build(row, level):
            far = place_ref[...] - (iota((8, 512), 0) + level).astype(F32)
            in_l = jnp.maximum(1.0 - jnp.abs(far), 0.0)
            for l in range(8):
                hi, lo = split(in_l[l:l + 1] * in_x_ref[...])
                at = pl.ds(row + 32 * l, 32)
                ahi_ref[at] = hi
                alo_ref[at] = lo

        build(0, 0)
        build(256, 8)
        table = table_ref[:, lanes(start, 0, 512)]
        both = mm(table, ahi_ref[0:512])
        sum_ref[...] = both[:128] + both[128:] + mm(table[:128], alo_ref[0:512])

        def gather(at, rows, level):
            build(pl.multiple_of(32 * level, 256), level)
            table = table_ref[:, at]
            both = mm(table, ahi_ref[rows])
            sum_ref[...] += both[:128] + both[128:] + mm(table[:128], alo_ref[rows])

        more(old_start, old_rest, lambda at, rows, level: adjoint(1 - slot, at, rows))
        more(start, rest, gather)

        for j in range(4):
            at = slice(128 * j, 128 * j + 128)
            get = lambda ch: obs_ref[sources[j], pl.ds(ch * 4 + parts[j], 1), :]
            dep = jnp.sum(sum_ref[:, at] * in_y_ref[:, at], 0, keepdims=True) - get(3)
            dep_ref[sources[j], pl.ds(parts[j], 1), :] = dep
            hi, lo = split(in_y_ref[:, at] * (dep * get(4)))
            spread_ref[0:128, at] = hi
            spread_ref[128:256, at] = lo
        return start, rest

    def two_groups(i, before):
        return one_group(2 * i + 1, 1, one_group(2 * i, 0, before))

    start, rest = lax.fori_loop(0, (groups + 1) // 2, two_groups, (jnp.int32(0), jnp.int32(0)))
    adjoint(1, lanes(start, 0, 512), slice(0, 512))
    more(start, rest, lambda at, rows, level: adjoint(1, at, rows))
    adj_ref[...] = (acc_ref[0:128, 0:1024] + acc_ref[128:256, 0:1024] + acc_ref[256:384, 0:1024]).T


def stencil(order, table, obs):
    return pl.pallas_call(
        stencil_kernel,
        out_shape=(jax.ShapeDtypeStruct((32, 4, 128), F32), jax.ShapeDtypeStruct((1024, 128), F32)),
        in_specs=[pl.BlockSpec(memory_space=pltpu.SMEM)] + [pl.BlockSpec(memory_space=pltpu.VMEM)] * 2,
        out_specs=(pl.BlockSpec(memory_space=pltpu.VMEM),) * 2,
        scratch_shapes=[
            pltpu.VMEM((384, 1280), F32),
            pltpu.VMEM((1280, 512), BF16),
            pltpu.VMEM((1280, 512), BF16),
            pltpu.VMEM((1280, 512), BF16),
            pltpu.VMEM((1280, 512), BF16),
            pltpu.VMEM((8, 512), F32),
            pltpu.VMEM((32, 512), F32),
            pltpu.VMEM((128, 512), F32),
            pltpu.VMEM((128, 512), F32),
            pltpu.VMEM((256, 512), BF16),
            pltpu.VMEM((32, 16, 128), F32),
        ],
        compiler_params=pltpu.CompilerParams(vmem_limit_bytes=VMEM_LIMIT),
        name="stencil",
    )(order, table, obs)


def line_weights(fine, coarse):
    out = np.zeros((fine, coarse), np.float32)
    for f in range(fine):
        out[f, f // RATIO] += 1.0 - (f % RATIO) / RATIO
        out[f, f // RATIO + 1] += (f % RATIO) / RATIO
    return out


def tables():
    along = line_weights(128, 40)
    across = line_weights(32, 16)
    spread_y = np.concatenate([along.T, along.T], 0)
    gather_y = np.concatenate([along.T, along.T], 1)
    eye = np.eye(8, dtype=np.float32)
    block = np.kron(eye, across)
    spread_x = np.concatenate([block, block], 1)
    gather_x = np.concatenate([block.T, block.T], 1)
    return [jnp.asarray(t, BF16) for t in (spread_y, gather_y, spread_x, gather_x)]


def diffuse_rows(field, first, last):
    near = field[first - 1:last - 1] + field[first + 1:last + 1]
    mid = field[first:last]
    near = near + pltpu.roll(mid, 1, 1) + pltpu.roll(mid, 47, 1)
    return mid + NU * (near - 4.0 * mid)


def three(a, b_ref):
    hi, lo = split(a)
    return mm(jnp.concatenate([hi, lo, hi], 1), b_ref[...])

MESH = pl.DeviceIdType.MESH
GROUPS = 32
CHUNKS = 5
BLOCKS = 4


def tile_id(index, mem):
    return (index // 4, index % 4, mem)


def remote(src, dst, send, recv, device):
    return pltpu.make_async_remote_copy(src_ref=src, dst_ref=dst, send_sem=send, recv_sem=recv, device_id=device, device_id_type=MESH)


class Place:
    def __init__(self):
        self.tx, self.ty, self.mem = lax.axis_index("tx"), lax.axis_index("ty"), lax.axis_index("mem")
        self.core = self.mem % 2
        self.below = (lax.rem(self.tx + 1, 8), self.ty, self.mem)
        self.above = (lax.rem(self.tx + 7, 8), self.ty, self.mem)
        self.right = (self.tx, lax.rem(self.ty + 1, 4), self.mem)
        self.left = (self.tx, lax.rem(self.ty + 3, 4), self.mem)
        self.twin = (self.tx, self.ty, self.mem + 1 - 2 * self.core)
        self.across = (self.tx, self.ty, lax.rem(self.mem + 2, 4))

    def along_ty(self, d):
        return (self.tx, lax.rem(self.ty + d, 4), self.mem)

    def along_tx(self, d):
        return (lax.rem(self.tx + d, 8), self.ty, self.mem)

    def greet(self, meanwhile):
        barrier = pltpu.get_barrier_semaphore()
        others = [self.along_tx(d) for d in range(1, 8)] + [self.along_ty(d) for d in range(1, 4)] + [self.twin, self.across]
        for other in others:
            pl.semaphore_signal(barrier, inc=1, device_id=other, device_id_type=MESH)
        meanwhile()
        pl.semaphore_wait(barrier, len(others))


class Exchange:
    def __init__(self, place, src, mid, dst, send, recv, own):
        self.place, self.src, self.mid, self.dst, self.send, self.recv, self.own = place, src, mid, dst, send, recv, own

    def first(self, d):
        other = self.place.along_ty(d)
        return remote(self.src.at[:, other[1]], self.mid.at[self.place.ty], self.send.at[d - 1], self.recv.at[d - 1], other)

    def second(self, d):
        other = self.place.along_tx(d)
        return remote(self.mid.at[:, other[0]], self.dst.at[self.place.tx], self.send.at[d + 2], self.recv.at[d + 2], other)

    def keep(self, at):
        if at == 0:
            return pltpu.make_async_copy(self.src.at[:, self.place.ty], self.mid.at[self.place.ty], self.own.at[0])
        return pltpu.make_async_copy(self.mid.at[:, self.place.tx], self.dst.at[self.place.tx], self.own.at[1])

    def start(self):
        self.keep(0).start()
        for d in range(1, 4):
            self.first(d).start()

    def turn(self):
        self.keep(0).wait()
        for d in range(1, 4):
            self.first(d).wait()
        self.keep(1).start()
        for d in range(1, 8):
            self.second(d).start()

    def wait(self):
        self.keep(1).wait()
        for d in range(1, 8):
            self.second(d).wait()


class MemSum:
    def __init__(self, place, part, total, half, got, far, send, recv):
        self.place, self.part, self.total = place, part, total
        self.half, self.got, self.far, self.send, self.recv = half, got, far, send, recv

    def mine(self, b):
        return pl.ds(8 * b + 4 * self.place.core, 4)

    def near(self, b):
        return remote(self.part.at[pl.ds(8 * b + 4 - 4 * self.place.core, 4)], self.got.at[b], self.send.at[0, b], self.recv.at[0, b], self.place.twin)

    def over(self, b):
        return remote(self.half.at[b], self.far.at[b], self.send.at[1, b], self.recv.at[1, b], self.place.across)

    def back(self, b):
        return remote(self.total.at[self.mine(b)], self.total.at[self.mine(b)], self.send.at[2, b], self.recv.at[2, b], self.place.twin)

    def second(self, b):
        self.near(b).wait()
        self.half[b] = self.part[self.mine(b)] + self.got[b]
        self.over(b).start()

    def third(self, b, extra):
        self.over(b).wait()
        self.total[self.mine(b)] = self.half[b] + self.far[b] + extra(self.mine(b))
        self.back(b).start()

    def last(self, b):
        self.back(b).wait()


MEM_SCRATCH = [pltpu.VMEM((BLOCKS, 4, 32, 128), F32)] * 3 + [pltpu.SemaphoreType.DMA((3, BLOCKS))] * 2


def route_ranks(cnt_ref, owner_ref, col_ref, lev_ref, frac_ref, inn_ref, rinv_ref, tgt_ref, high_ref, low_ref, term_ref):
    rows, wide = owner_ref.shape
    place = iota((rows, wide), 0) * wide + iota((rows, wide), 1)
    live = place < cnt_ref[0]
    owner = jnp.where(live, owner_ref[...], GROUPS)
    level = lev_ref[...]
    key = (owner * 32 + level).astype(F32)
    turned = jnp.concatenate([key, key], 0).T
    earlier = iota((wide, wide), 0) < iota((wide, wide), 1)
    one_if = lambda cond: jnp.where(cond, 1.0, 0.0).astype(BF16)
    owners = [one_if(iota((GROUPS, wide), 0) == owner[c:c + 1]) for c in range(rows)]
    levels = [one_if(iota((32, wide), 0) == level[c:c + 1]) for c in range(rows)]
    running = jnp.zeros((GROUPS, 32), F32)
    starts = []
    for c in range(rows):
        starts.append(running)
        running = running + mm(owners[c], levels[c], NT)
    lower = one_if(iota((32, 32), 0) < iota((32, 32), 1))
    hi, lo = split(running)
    offset = mm(hi, lower) + mm(lo, lower)
    ranks = []
    for c in range(rows):
        hi, lo = split(offset + starts[c])
        both = mm(jnp.concatenate([hi, lo], 0), levels[c])
        same = jnp.where((turned[:, c:c + 1] == key[c:c + 1]) & earlier, 1.0, 0.0)
        at = (both[:GROUPS] + both[GROUPS:]) * owners[c].astype(F32)
        ranks.append(jnp.sum(at, 0, keepdims=True) + jnp.sum(same, 0, keepdims=True))
    rank = jnp.where(live, jnp.concatenate(ranks, 0).astype(jnp.int32), 0)
    tgt_ref[...] = jnp.where(live, owner * 512 + rank, -1)
    high_ref[...] = jnp.where(live, rank // 128 * GROUPS + owner, -1)
    low_ref[...] = rank % 128
    base = (lev_ref[...] * 4096 + col_ref[...]).astype(F32)
    for at, v in ((3, inn_ref[...]), (4, rinv_ref[...]), (5, base)):
        hi, lo = split(v)
        term_ref[2 * at] = hi.astype(F32)
        term_ref[2 * at + 1] = lo.astype(F32)
    for at in range(3):
        for r in range(rows):
            hi, lo = split(frac_ref[at:at + 1, wide * r:wide * (r + 1)])
            term_ref[2 * at, r:r + 1] = hi.astype(F32)
            term_ref[2 * at + 1, r:r + 1] = lo.astype(F32)


def route_slots(start, count, high_ref, low_ref, term_ref, acc_ref):
    def one(c, carry):
        def line(ref, *at):
            rows = ref[(*at, pl.ds(pl.multiple_of(8 * c, 8), 8), slice(None))]
            return jnp.concatenate([rows[r:r + 1] for r in range(8)], 1)

        hit = jnp.where(iota((128, 1024), 0) == line(high_ref), 1.0, 0.0).astype(BF16)
        lane = jnp.where(iota((128, 1024), 0) == line(low_ref), 1.0, 0.0).astype(BF16)
        for ch in range(6):
            stack = jnp.concatenate([lane * line(term_ref, 2 * ch + t).astype(BF16) for t in range(2)], 0)
            acc_ref[:, 256 * ch:256 * ch + 256] += mm(hit, stack, NT)
        return carry

    lax.fori_loop(start, start + count, one, 0)


def route_out(acc_ref, out_ref):
    for ch in range(6):
        full = acc_ref[:, 256 * ch:256 * ch + 128] + acc_ref[:, 256 * ch + 128:256 * ch + 256]
        for q in range(4):
            rows = full[q * GROUPS:(q + 1) * GROUPS].reshape(8, 4, 128)
            out_ref[:, :, ch * 4 + q, :] = rows


def unroute(tgt_ref, ret, out_ref):
    rows = tgt_ref.shape[0]
    hi, lo = split(ret.T)
    table = jnp.concatenate([hi, lo], 0)
    for c in range(0, rows, 2):
        tgt = jnp.concatenate([tgt_ref[c:c + 1], tgt_ref[c + 1:c + 2]], 1)
        hit = jnp.where(iota((128, 256), 0) == tgt // 128, 1.0, 0.0).astype(BF16)
        picked = mm(table, hit)
        picked = picked[:128] + picked[128:]
        row = jnp.sum(jnp.where((iota((128, 256), 0) == tgt % 128) & (tgt >= 0), picked, 0.0), 0, keepdims=True)
        out_ref[c:c + 1] = row[:, :128]
        out_ref[c + 1:c + 2] = row[:, 128:]


def diffuse_rows(field):
    near = field[:-2] + field[2:]
    mid = field[1:-1]
    near = near + pltpu.roll(mid, 1, 1) + pltpu.roll(mid, 47, 1)
    return mid + NU * (near - 4.0 * mid)


def mixing(lv):
    tiled = jnp.concatenate([jnp.concatenate([lv] * 4, 1)] * 4, 0)
    return jnp.where(iota((128, 128), 0) // 32 == iota((128, 128), 1) // 32, tiled, 0.0)


def three(a, b):
    hi, lo = split(a)
    bhi, blo = split(b)
    return mm(jnp.concatenate([hi, lo, hi], 1), jnp.concatenate([bhi, bhi, blo], 0))


def forward_kernel(
    cnt_ref, owner_ref, col_ref, lev_ref, frac_ref, inn_ref, rinv_ref, alpha_ref, pert_hbm, bg_ref, static_ref, lv_ref, sy_ref, sx_ref,
    table_ref, obs_ref, order_ref, tgt_ref,
    inc_ref, halo_ref, fromleft_ref, fromright_ref, mine_ref, pert_ref, turn_ref, part_ref, out_ref, mid_ref, high_ref, low_ref, term_ref, acc_ref,
    half_ref, got_ref, far_ref, msend, mrecv,
    xsend, xrecv, ysend, yrecv, osend, orecv, around, own,
):
    place = Place()

    def x_copies(g):
        lanes = pl.ds(pl.multiple_of(g * 128, 128), 128)
        return (
            remote(alpha_ref.at[4:8, :, lanes], halo_ref.at[g, 0:4, 8:40], xsend.at[0, g], xrecv.at[0, g], place.below),
            remote(alpha_ref.at[0:5, :, lanes], halo_ref.at[g, 4:9, 8:40], xsend.at[1, g], xrecv.at[1, g], place.above),
        )

    y_copies = (
        remote(alpha_ref.at[:, 24:32], fromleft_ref, ysend.at[0, CHUNKS], yrecv.at[0, CHUNKS], place.right),
        remote(alpha_ref.at[:, 0:8], fromright_ref, ysend.at[1, CHUNKS], yrecv.at[1, CHUNKS], place.left),
    )

    def corner_copies(g):
        return (
            remote(halo_ref.at[g, :, 32:40], halo_ref.at[g, :, 0:8], ysend.at[0, g], yrecv.at[0, g], place.right),
            remote(halo_ref.at[g, :, 8:16], halo_ref.at[g, :, 40:48], ysend.at[1, g], yrecv.at[1, g], place.left),
        )

    own_copy = pltpu.make_async_copy(alpha_ref, mine_ref, own.at[0])
    pert_copy = pltpu.make_async_copy(pert_hbm, pert_ref, own.at[1])
    exchange = Exchange(place, out_ref, mid_ref, obs_ref, osend, orecv, around)
    total = MemSum(place, part_ref, inc_ref, half_ref, got_ref, far_ref, msend, mrecv)

    def meanwhile():
        own_copy.start()
        pert_copy.start()
        turn_ref[...] = jnp.zeros_like(turn_ref)
        acc_ref[...] = jnp.zeros_like(acc_ref)
        part_ref[...] = jnp.zeros_like(part_ref)

    place.greet(meanwhile)

    def begin(g, carry):
        for copy in x_copies(g):
            copy.start()
        return carry

    lax.fori_loop(0, CHUNKS, begin, 0)
    for copy in y_copies:
        copy.start()
    route_ranks(cnt_ref, owner_ref, col_ref, lev_ref, frac_ref, inn_ref, rinv_ref, tgt_ref, high_ref, low_ref, term_ref)
    mix = mixing(lv_ref[...]).T
    own_copy.wait()
    pert_copy.wait()
    for copy in y_copies:
        copy.wait()

    def sideways(g):
        for copy in x_copies(g):
            copy.wait()
        for copy in corner_copies(g):
            copy.start()

    def smooth(g):
        for copy in corner_copies(g):
            copy.wait()
        lanes = pl.ds(pl.multiple_of(g * 128, 128), 128)
        center = jnp.concatenate([fromleft_ref[:, :, lanes], mine_ref[:, :, lanes], fromright_ref[:, :, lanes]], 1)
        field = jnp.concatenate([halo_ref[g, 0:4], center, halo_ref[g, 4:9]], 0)
        for step in range(4):
            field = diffuse_rows(field)
        field = three(field[:, 8:48].reshape(9 * 40, 128), mix).reshape(9, 40, 128)
        for a in range(9):
            hi, lo = split(field[a])
            turn_ref[:, a, :] = mm(jnp.concatenate([hi, lo], 0), sy_ref[...], TN)
        for b in range(BLOCKS):
            at = slice(8 * b, 8 * b + 8)
            sums = part_ref[at]
            for k in range(4):
                hi, lo = split(turn_ref[32 * k + 8 * b:32 * k + 8 * b + 8].reshape(128, 128))
                fine = mm(sx_ref[...], jnp.concatenate([hi, lo], 0)).reshape(8, 32, 128)
                sums = sums + fine * pert_ref[4 * g + k, at].astype(F32)
            part_ref[at] = sums

    sideways(0)
    route_slots(0, 4, high_ref, low_ref, term_ref, acc_ref)
    sideways(1)
    route_slots(4, 4, high_ref, low_ref, term_ref, acc_ref)
    sideways(2)
    route_out(acc_ref, out_ref)
    exchange.start()

    def both(g, carry):
        @pl.when(g == 2)
        def _():
            exchange.turn()

        smooth(g)

        @pl.when(g < CHUNKS - 3)
        def _():
            sideways(g + 3)

        return carry

    lax.fori_loop(0, CHUNKS, both, 0)

    extra = lambda at: bg_ref[at] * static_ref[at]
    for b in range(BLOCKS):
        total.near(b).start()
    for b in range(BLOCKS):
        total.second(b)
    exchange.wait()
    order_ref[...] = chunk_order(obs_ref[...].reshape(GROUPS, 24, 128))
    for b in range(BLOCKS):
        total.third(b, extra)
    for b in range(BLOCKS):
        total.last(b)
        hi, lo = split(inc_ref[8 * b:8 * b + 8].reshape(256, 128).T)
        table_ref[0:128, 256 * b:256 * b + 256] = hi
        table_ref[128:256, 256 * b:256 * b + 256] = lo
    table_ref[:, 1024:1280] = jnp.zeros((256, 256), BF16)


VMEM = pl.BlockSpec(memory_space=pltpu.VMEM)
SMEM = pl.BlockSpec(memory_space=pltpu.SMEM)
ANY = pl.BlockSpec(memory_space=pl.ANY)
DMA = pltpu.SemaphoreType.DMA


def forward(cnt, owner, col, lev, frac, inn, rinv, alpha, pert, bg, static, lv, sy, sx):
    return pl.pallas_call(
        forward_kernel,
        out_shape=(
            jax.ShapeDtypeStruct((256, 1280), BF16),
            jax.ShapeDtypeStruct((8, 4, 24, 128), F32),
            jax.ShapeDtypeStruct((8, 128), jnp.int32),
            jax.ShapeDtypeStruct((64, 128), jnp.int32),
        ),
        in_specs=[SMEM] + [VMEM] * 6 + [ANY] * 2 + [VMEM] * 5,
        out_specs=(VMEM,) * 4,
        scratch_shapes=[
            pltpu.VMEM((32, 32, 128), F32),
            pltpu.VMEM((CHUNKS, 9, 48, 128), F32),
            pltpu.VMEM((8, 8, 640), F32),
            pltpu.VMEM((8, 8, 640), F32),
            pltpu.VMEM((8, 32, 640), F32),
            pltpu.VMEM(pert.shape, BF16),
            pltpu.VMEM((128, 16, 128), F32),
            pltpu.VMEM((32, 32, 128), F32),
            pltpu.VMEM((8, 4, 24, 128), F32),
            pltpu.VMEM((4, 8, 24, 128), F32),
            pltpu.VMEM((64, 128), jnp.int32),
            pltpu.VMEM((64, 128), jnp.int32),
            pltpu.VMEM((12, 64, 128), F32),
            pltpu.VMEM((128, 1536), F32),
        ] + MEM_SCRATCH + [DMA((2, CHUNKS))] * 2 + [DMA((2, CHUNKS + 1))] * 2 + [DMA((10,))] * 2 + [DMA((2,)), DMA((2,))],
        compiler_params=pltpu.CompilerParams(vmem_limit_bytes=VMEM_LIMIT, collective_id=0, has_side_effects=True),
        name="forward",
    )(cnt, owner, col, lev, frac, inn, rinv, alpha, pert, bg, static, lv, sy, sx)


def backward_kernel(
    adj_ref, dep_ref, tgt_ref, pert_hbm, lv_ref, gy_ref, gx_ref,
    grad_ref, full_ref, depout_ref,
    pert_ref, turn_ref, wide_ref, fromleft_ref, fromright_ref, fromabove_ref, frombelow_ref, mid_ref, ret_ref,
    half_ref, got_ref, far_ref, msend, mrecv,
    xsend, xrecv, ysend, yrecv, osend, orecv, around, own,
):
    place = Place()

    def y_copies(g):
        return (
            remote(wide_ref.at[g, :, 40:48], fromleft_ref.at[g], ysend.at[0, g], yrecv.at[0, g], place.right),
            remote(wide_ref.at[g, :, 0:8], fromright_ref.at[g], ysend.at[1, g], yrecv.at[1, g], place.left),
        )

    def x_copies(g):
        return (
            remote(wide_ref.at[g, 12:17, 8:40], fromabove_ref.at[g], xsend.at[0, g], xrecv.at[0, g], place.below),
            remote(wide_ref.at[g, 0:4, 8:40], frombelow_ref.at[g], xsend.at[1, g], xrecv.at[1, g], place.above),
        )

    pert_copy = pltpu.make_async_copy(pert_hbm, pert_ref, own.at[0])
    exchange = Exchange(place, dep_ref, mid_ref, ret_ref, osend, orecv, around)
    total = MemSum(place, adj_ref, full_ref, half_ref, got_ref, far_ref, msend, mrecv)

    place.greet(pert_copy.start)
    for b in range(BLOCKS):
        total.near(b).start()
    for b in range(BLOCKS):
        total.second(b)
    exchange.start()
    pert_copy.wait()

    def block(b, start, count):
        fine_adj = full_ref[8 * b:8 * b + 8]

        def member(k, carry):
            fine = fine_adj * pert_ref[k, 8 * b:8 * b + 8].astype(F32)
            hi, lo = split(fine.reshape(256, 128))
            turn_ref[pl.ds(k * 32 + 8 * b, 8)] = mm(gx_ref[...], jnp.concatenate([hi, lo], 0)).reshape(8, 16, 128)
            return carry

        if count == 4:
            for k in range(4):
                member(start + k, 0)
        else:
            lax.fori_loop(start, start + count, member, 0, unroll=4)

    for s in range(BLOCKS + 1):
        if s < BLOCKS:
            total.third(s, lambda at: 0.0)
        if s >= 1:
            total.last(s - 1)
            if s < BLOCKS:
                block(s - 1, 0, 20)

    exchange.turn()
    mix = mixing(lv_ref[...])

    def smooth(g, carry):
        block(BLOCKS - 1, 4 * g, 4)
        rows = []
        for a in range(9):
            hi, lo = split(turn_ref[pl.ds(pl.multiple_of(g * 128, 128), 128), a, :])
            rows.append(mm(gy_ref[...], jnp.concatenate([hi, lo], 1), NT))
        field = three(jnp.concatenate(rows, 0), mix).reshape(9, 40, 128)
        field = jnp.concatenate([jnp.zeros((9, 8, 128), F32), field], 1)
        for step in range(4):
            two = jnp.zeros((2, 48, 128), F32)
            field = diffuse_rows(jnp.concatenate([two, field, two], 0))
        wide_ref[g] = field
        for copy in y_copies(g):
            copy.start()
        return carry

    def lengthways(g, carry):
        for copy in y_copies(g):
            copy.wait()
        wide_ref[g, :, 8:16] += fromleft_ref[g]
        wide_ref[g, :, 32:40] += fromright_ref[g]
        for copy in x_copies(g):
            copy.start()
        return carry

    def both(g, carry):
        smooth(g, carry)
        return lengthways(g - 1, carry)

    smooth(0, 0)
    lax.fori_loop(1, CHUNKS, both, 0)
    lengthways(CHUNKS - 1, 0)

    exchange.wait()
    unroute(tgt_ref, ret_ref[...].reshape(128, 128), depout_ref)
    for g in range(CHUNKS):
        for copy in x_copies(g):
            copy.wait()
        lanes = slice(128 * g, 128 * g + 128)
        grad_ref[:, :, lanes] = wide_ref[g, 4:12, 8:40]
        grad_ref[0:5, :, lanes] += fromabove_ref[g]
        grad_ref[4:8, :, lanes] += frombelow_ref[g]


def backward(adj, dep, tgt, pert, lv, gy, gx):
    return pl.pallas_call(
        backward_kernel,
        out_shape=(
            jax.ShapeDtypeStruct((8, 32, 640), F32),
            jax.ShapeDtypeStruct((32, 32, 128), F32),
            jax.ShapeDtypeStruct(tgt.shape, F32),
        ),
        in_specs=[VMEM] * 3 + [ANY] + [VMEM] * 3,
        out_specs=(VMEM,) * 3,
        scratch_shapes=[
            pltpu.VMEM(pert.shape, BF16),
            pltpu.VMEM((640, 16, 128), F32),
            pltpu.VMEM((CHUNKS, 17, 48, 128), F32),
            pltpu.VMEM((CHUNKS, 17, 8, 128), F32),
            pltpu.VMEM((CHUNKS, 17, 8, 128), F32),
            pltpu.VMEM((CHUNKS, 5, 32, 128), F32),
            pltpu.VMEM((CHUNKS, 4, 32, 128), F32),
            pltpu.VMEM((4, 8, 4, 128), F32),
            pltpu.VMEM((8, 4, 4, 128), F32),
        ] + MEM_SCRATCH + [DMA((2, CHUNKS))] * 4 + [DMA((10,))] * 2 + [DMA((2,)), DMA((1,))],
        compiler_params=pltpu.CompilerParams(vmem_limit_bytes=VMEM_LIMIT, collective_id=1, has_side_effects=True),
        name="backward",
    )(adj, dep, tgt, pert, lv, gy, gx)


def finish_kernel(alpha_ref, back_ref, bg_ref, static_ref, adj_ref, dep_ref, grad_ref, gstat_ref, out_ref):
    grad_ref[...] = alpha_ref[...] + back_ref[...]
    gstat_ref[...] = static_ref[...] + bg_ref[...] * adj_ref[...]
    out_ref[...] = dep_ref[...]


def finish(alpha, back, bg, static, adj, dep):
    return pl.pallas_call(
        finish_kernel,
        out_shape=tuple(jax.ShapeDtypeStruct(a.shape, F32) for a in (alpha, static, dep)),
        in_specs=[VMEM] * 6,
        out_specs=(VMEM,) * 3,
        compiler_params=pltpu.CompilerParams(vmem_limit_bytes=VMEM_LIMIT),
        name="finish",
    )(alpha, back, bg, static, adj, dep)


def per_device(alpha, lv_sqrt, ens_pert, bg_sigma, static_ctrl, obs_owner, obs_column, obs_level, obs_frac, innovation, obs_rinv, obs_count):
    spread_y, gather_y, spread_x, gather_x = tables()
    shape = (64, 128)
    table, incoming, order, target = forward(
        obs_count, obs_owner.reshape(shape), obs_column.reshape(shape), obs_level.reshape(shape), obs_frac,
        innovation.reshape(shape), obs_rinv.reshape(shape), alpha, ens_pert, bg_sigma, static_ctrl, lv_sqrt, spread_y, spread_x,
    )
    departure, adjoint = stencil(order, table, incoming.reshape(GROUPS, 24, 128))
    back, adjoint, departures = backward(adjoint.reshape(32, 32, 128), departure.reshape(8, 4, 4, 128), target, ens_pert, lv_sqrt, gather_y, gather_x)
    grad_alpha, grad_static, departures = finish(alpha, back, bg_sigma, static_ctrl, adjoint, departures)
    return grad_alpha, grad_static, departures.reshape(-1)


def solution(mesh):
    placed = (
        P("tx", "ty", "mem"),
        P(),
        P("mem", None, "tx", "ty"),
        P(None, "tx", "ty"),
        P(None, "tx", "ty"),
        P(("tx", "ty", "mem"), None),
        P(("tx", "ty", "mem")),
        P(("tx", "ty", "mem")),
        P(None, ("tx", "ty", "mem")),
        P(("tx", "ty", "mem")),
        P(("tx", "ty", "mem")),
        P(("tx", "ty", "mem")),
    )
    return jax.shard_map(
        per_device,
        mesh=mesh,
        in_specs=placed,
        out_specs=(P("tx", "ty", "mem"), P(None, "tx", "ty"), P(("tx", "ty", "mem"))),
        check_vma=False,
    )
```
